256 devices in a mesh: samp: 32 (over y_hi, z, core), par: 8 (over y_lo, x).
Axes of the slice: x: 4, y: 4 (y_hi: 2, y_lo: 2; y = y_hi * 2 + y_lo), z: 8, core: 2. Of those that a mesh axis runs over, the one named last changes fastest.
Arguments:
- jacobian: float32 [256, 65536], P('samp', 'par'), may hold values from -32 to 32
- energies: float32 [256], P('samp'), may hold values from -20 to 24
Outputs:
- update: float32 [65536], P('par')
- coeffs: float32 [256], P('samp')
The draws below stay inside these ranges and needn't reach their ends.
All inputs are finite; a program needn't handle non-finite values.
Results may differ from the reference program's by a relative error of at most 0.0029.
Values may be sent and summed in bfloat16 or wider, within the bound.
A program may use at most 64 MiB of HBM per device.

```python
import math
import jax
import jax.numpy as jnp
from jax import lax

P_SIZE = 65536
ITERS = 3
S = 256


def draw_jacobian(key, part):
    key = jax.random.fold_in(key, 11)
    keys = jax.random.split(key, 4)
    positions = jnp.arange(S, dtype=jnp.float32)
    ramp = 1.0 + 2.0 * positions / (S - 1)
    row_scale = jnp.exp(jax.random.uniform(keys[0], (S, 1), jnp.float32, math.log(0.5), math.log(1.5)))
    col_scale = jnp.exp(jax.random.uniform(keys[1], (1, P_SIZE), jnp.float32, math.log(0.5), math.log(1.5)))
    offset = jnp.clip(jax.random.normal(keys[2], (1, P_SIZE), jnp.float32), -3.0, 3.0)
    noise = jnp.clip(jax.random.normal(keys[3], (S, P_SIZE), jnp.float32), -4.0, 4.0)
    return offset + ramp[:, None] * row_scale * col_scale * noise


def draw_energies(key, part):
    key = jax.random.fold_in(key, 12)
    keys = jax.random.split(key, 2)
    positions = jnp.arange(S, dtype=jnp.float32)
    ramp = 1.0 + 2.0 * positions / (S - 1)
    spread = jnp.exp(jax.random.uniform(keys[0], (S,), jnp.float32, math.log(0.5), math.log(1.5)))
    noise = jnp.clip(jax.random.normal(keys[1], (S,), jnp.float32), -4.0, 4.0)
    base_level = 3.0
    return base_level + ramp * spread * noise


def setup_inputs(seed: int = 0) -> dict:
    key_list = jax.random.split(jax.random.key(seed), 3)
    return {
        "jacobian": draw_jacobian(jax.random.fold_in(key_list[2], 71), 0),
        "energies": draw_energies(jax.random.fold_in(key_list[2], 71), 0),
    }


def operator_apply(scaled, vector):
    column_image = jnp.dot(vector, scaled, precision=lax.Precision.HIGHEST, preferred_element_type=jnp.float32)
    row_image = jnp.dot(scaled, column_image, precision=lax.Precision.HIGHEST, preferred_element_type=jnp.float32)
    return row_image + 0.05 * vector

def reference(jacobian, energies):
    mean_col = lax.optimization_barrier(jnp.sum(jacobian, axis=0)) / S
    scaled = ((jacobian - mean_col[None, :]) / math.sqrt(P_SIZE)).astype(jnp.bfloat16)
    right_side = jnp.sum(energies) / S - energies
    coeffs = jnp.zeros_like(right_side)
    residual = right_side
    direction = right_side
    norm_now = jnp.sum(residual * residual)
    for turn_index in range(ITERS):
        image = operator_apply(scaled, direction)
        step_size = norm_now / jnp.sum(direction * image)
        coeffs = coeffs + step_size * direction
        residual = residual - step_size * image
        norm_next = jnp.sum(residual * residual)
        direction = residual + norm_next / norm_now * direction
        norm_now = norm_next
    update = jnp.dot(coeffs, scaled, precision=lax.Precision.HIGHEST, preferred_element_type=jnp.float32)
    return (update, coeffs)
```

```python
import functools

import jax
import jax.numpy as jnp
from jax import lax
from jax.experimental import pallas as pl
from jax.experimental.pallas import tpu as pltpu
from jax.sharding import PartitionSpec as P

P_SIZE = 65536
ITERS = 3
SHIFT = 0.05
CORES = 2
Y_HI = 2
LANES = 128
MESH = pl.DeviceIdType.MESH


def total_rows(block):
    return jnp.sum(block, axis=0, keepdims=True)


def total_lanes(block):
    return jnp.sum(block, axis=1, keepdims=True)


def kernel(
    samp,
    par,
    jac,
    energies,
    update,
    coeffs,
    jbuf,
    ebuf,
    eown,
    scaled_ref,
    gpart,
    rs,
    ar,
    gram,
    upiece,
    send,
    recv,
):
    depth = samp // (CORES * Y_HI)
    plane = CORES * Y_HI * par
    rows, width = jbuf.shape[1], jbuf.shape[2]
    count = samp * rows

    s = lax.axis_index("samp")
    p = lax.axis_index("par")
    core = lax.rem(s, CORES)
    z = lax.rem(s // CORES, depth)
    y_hi = s // (CORES * depth)
    a = (y_hi * par + p) * CORES + core

    def samp_peer(k):
        return lax.rem(s + k, samp), p

    def plane_peer(k):
        there = lax.rem(a + k, plane)
        there_core = lax.rem(there, CORES)
        there_p = lax.rem(there // CORES, par)
        there_y = there // (CORES * par)
        return there, ((there_y * depth + z) * CORES + there_core, there_p)

    def depth_peer(k):
        there = lax.rem(z + k, depth)
        return (y_hi * depth + there) * CORES + core, p

    def each(first, last, body):
        def step(k, carry):
            body(k)
            return carry

        lax.fori_loop(first, last, step, 0)

    def remote(src, dst, which, device):
        return pltpu.make_async_remote_copy(
            src_ref=src,
            dst_ref=dst,
            send_sem=send.at[which],
            recv_sem=recv.at[which],
            device_id=device,
            device_id_type=MESH,
        )

    def landed(block, which):
        pltpu.make_async_copy(block, block, recv.at[which]).wait()

    def sent(block, which):
        pltpu.make_async_copy(block, block, send.at[which]).wait()

    barrier = pltpu.get_barrier_semaphore()

    def greet(device):
        pl.semaphore_signal(barrier, inc=1, device_id=device, device_id_type=MESH)

    each(1, samp, lambda k: greet(samp_peer(k)))

    def greet_plane(k):
        there_p = lax.rem(p + 1 + k // (CORES * Y_HI), par)
        rest = lax.rem(k, CORES * Y_HI)
        there_s = ((rest // CORES) * depth + z) * CORES + lax.rem(rest, CORES)
        greet((there_s, there_p))

    each(0, CORES * Y_HI * (par - 1), greet_plane)

    own = pltpu.make_async_copy(
        jac.at[:, pl.ds(pl.multiple_of(s * width, width), width)], jbuf.at[s], recv.at[0]
    )
    own.start()
    lane = lax.broadcasted_iota(jnp.int32, (1, LANES), 1)
    offset = lax.rem(s * rows, LANES)
    mine = jnp.zeros((1, LANES), jnp.float32)
    for r in range(rows):
        mine = jnp.where(lane == offset + r, energies[r], mine)
    eown[...] = mine
    ebuf[s] = mine

    pl.semaphore_wait(barrier, samp - 1 + CORES * Y_HI * (par - 1))

    def exchange(k):
        there, there_p = samp_peer(k)
        remote(
            jac.at[:, pl.ds(pl.multiple_of(there * width, width), width)],
            jbuf.at[s],
            0,
            (there, there_p),
        ).start()

    each(1, samp, exchange)
    each(1, samp, lambda k: remote(eown, ebuf.at[s], 1, samp_peer(k)).start())

    landed(jbuf, 0)
    block = jbuf[...].reshape(count, width)
    mean_col = total_rows(block) / count
    scaled = ((block - mean_col) * (1.0 / P_SIZE**0.5)).astype(jnp.bfloat16)
    scaled_ref[...] = scaled
    part = lax.dot_general(
        scaled, scaled, (((1,), (1,)), ((), ())), preferred_element_type=jnp.float32
    )
    gpart[...] = part.reshape(gpart.shape)

    def scatter(k):
        there, device = plane_peer(k)
        remote(gpart.at[there], rs.at[a], 2, device).start()

    each(1, plane, scatter)
    rs[a] = gpart[a]

    landed(ebuf.at[pl.ds(0, samp - 1)], 1)
    per = LANES // rows
    level = jnp.concatenate(
        [jnp.sum(ebuf[i * per : (i + 1) * per], axis=0) for i in range(samp // per)], axis=1
    )
    right_row = total_lanes(level) / count - level
    diagonal = lax.broadcasted_iota(jnp.int32, (count, count), 0) == lax.broadcasted_iota(
        jnp.int32, (count, count), 1
    )
    right_col = total_lanes(jnp.where(diagonal, right_row, 0.0))

    landed(rs.at[pl.ds(0, plane - 1)], 2)
    ar[z] = jnp.sum(rs[...], axis=0)
    each(1, depth, lambda k: remote(ar.at[z], ar.at[z], 3, depth_peer(k)).start())
    landed(ar.at[pl.ds(0, depth - 1)], 3)
    gram[a] = jnp.sum(ar[...], axis=0)
    each(1, plane, lambda k: remote(gram.at[a], gram.at[a], 4, plane_peer(k)[1]).start())
    landed(gram.at[pl.ds(0, plane - 1)], 4)

    g = gram[...].reshape(count, count)
    d_row, d_col = right_row, right_col
    r_row, r_col = right_row, right_col
    c_row, c_col = jnp.zeros_like(right_row), jnp.zeros_like(right_col)
    rr = total_lanes(r_row * r_row)
    for turn in range(ITERS):
        image_row = total_rows(g * d_col) + SHIFT * d_row
        size = rr / total_lanes(d_row * image_row)
        c_row = c_row + size * d_row
        c_col = c_col + size * d_col
        if turn == ITERS - 1:
            break
        image_col = total_lanes(g * d_row) + SHIFT * d_col
        r_row = r_row - size * image_row
        r_col = r_col - size * image_col
        fresh = total_lanes(r_row * r_row)
        ratio = fresh / rr
        d_row = r_row + ratio * d_row
        d_col = r_col + ratio * d_col
        rr = fresh

    upiece[s] = total_rows(scaled_ref[...].astype(jnp.float32) * c_col)
    each(1, samp, lambda k: remote(upiece.at[s], upiece.at[s], 5, samp_peer(k)).start())

    here = s // per
    half = c_row[:, :LANES]
    for i in range(1, samp // per):
        half = jnp.where(here == i, c_row[:, i * LANES : (i + 1) * LANES], half)
    coeffs[...] = pltpu.roll(half, lax.rem(LANES - offset, LANES), 1)

    sent(jbuf.at[pl.ds(0, samp - 1)], 0)
    sent(ebuf.at[pl.ds(0, samp - 1)], 1)
    sent(rs.at[pl.ds(0, plane - 1)], 2)
    sent(ar.at[pl.ds(0, depth - 1)], 3)
    sent(gram.at[pl.ds(0, plane - 1)], 4)
    landed(upiece.at[pl.ds(0, samp - 1)], 5)
    update[...] = upiece[...]
    sent(upiece.at[pl.ds(0, samp - 1)], 5)


def solution(mesh):
    samp, par = mesh.shape["samp"], mesh.shape["par"]
    plane = CORES * Y_HI * par
    depth = samp // (CORES * Y_HI)

    def per_device(jacobian, energies):
        rows, columns = jacobian.shape
        width = columns // samp
        count = rows * samp
        update, coeffs = pl.pallas_call(
            functools.partial(kernel, samp, par),
            out_shape=(
                jax.ShapeDtypeStruct((samp, 1, width), jnp.float32),
                jax.ShapeDtypeStruct((1, LANES), jnp.float32),
            ),
            in_specs=[
                pl.BlockSpec(memory_space=pl.ANY),
                pl.BlockSpec(memory_space=pltpu.SMEM),
            ],
            out_specs=(
                pl.BlockSpec(memory_space=pltpu.VMEM),
                pl.BlockSpec(memory_space=pltpu.VMEM),
            ),
            scratch_shapes=[
                pltpu.VMEM((samp, rows, width), jnp.float32),
                pltpu.VMEM((samp, 1, LANES), jnp.float32),
                pltpu.VMEM((1, LANES), jnp.float32),
                pltpu.VMEM((count, width), jnp.bfloat16),
                pltpu.VMEM((plane, count // plane, count), jnp.float32),
                pltpu.VMEM((plane, count // plane, count), jnp.float32),
                pltpu.VMEM((depth, count // plane, count), jnp.float32),
                pltpu.VMEM((plane, count // plane, count), jnp.float32),
                pltpu.VMEM((samp, 1, width), jnp.float32),
                pltpu.SemaphoreType.DMA((6,)),
                pltpu.SemaphoreType.DMA((6,)),
            ],
            compiler_params=pltpu.CompilerParams(collective_id=0, has_side_effects=True),
        )(jacobian, energies)
        return update.reshape(columns), coeffs[0, :rows]

    return jax.shard_map(
        per_device,
        mesh=mesh,
        in_specs=(P("samp", "par"), P("samp")),
        out_specs=(P("par"), P("samp")),
        check_vma=False,
    )
```

```python
import functools

import jax
import jax.numpy as jnp
from jax import lax
from jax.experimental import pallas as pl
from jax.experimental.pallas import tpu as pltpu
from jax.sharding import PartitionSpec as P

P_SIZE = 65536
ITERS = 3
SHIFT = 0.05
CORES = 2
Y_HI = 2
Y_LO = 2
LANES = 128
VMEM_BYTES = 8 * 2**20
MESH = pl.DeviceIdType.MESH


def total_rows(block):
    return jnp.sum(block, axis=0, keepdims=True)


def total_lanes(block):
    return jnp.sum(block, axis=1, keepdims=True)


def each(count, body):
    def step(k, carry):
        body(k)
        return carry

    lax.fori_loop(0, count, step, 0)


def kernel(
    samp,
    par,
    jac,
    energies,
    out,
    jbuf,
    ebuf,
    eown,
    scaled_ref,
    gpart,
    rs,
    ar,
    top,
    low,
    upiece,
    send,
    recv,
):
    depth = samp // (CORES * Y_HI)
    xs = par // Y_LO
    ys = Y_HI * Y_LO
    chips = xs * ys
    rows, width = jbuf.shape[1], jbuf.shape[2]
    count = samp * rows
    half = count // 2
    per = LANES // rows

    s = lax.axis_index("samp")
    p = lax.axis_index("par")
    core = lax.rem(s, CORES)
    z = lax.rem(s // CORES, depth)
    y_hi = s // (CORES * depth)
    x = lax.rem(p, xs)
    y = y_hi * Y_LO + p // xs
    chip = y * xs + x
    rank = core * chips + chip
    right = pl.ds(half, half)

    def samp_at(there_z, y_off, core_off):
        there_y = lax.rem(y_hi + y_off, Y_HI)
        return (there_y * depth + there_z) * CORES + lax.rem(core + core_off, CORES)

    z_steps = sorted(range(depth), key=lambda k: -min(k, depth - k))

    def samp_peers(body):
        for z_off in z_steps:
            there_z = lax.rem(z + z_off, depth)

            def step(k):
                body(samp_at(there_z, lax.rem(k // CORES + 1, Y_HI), k + 1))

            each(CORES * Y_HI - (1 if z_off == 0 else 0), step)

    def ring(n):
        return lax.rem(2 + n * (7 - n) // 2, 4)

    def plane_chip(k):
        there_y = lax.rem(y + ring(k // xs), ys)
        return there_y, lax.rem(x + ring(lax.rem(k, xs)), xs)

    def on_chip(there_y, there_x, there_core):
        there_s = ((there_y // Y_LO) * depth + z) * CORES + there_core
        return there_s, lax.rem(there_y, Y_LO) * xs + there_x

    def remote(src, dst, which, device):
        return pltpu.make_async_remote_copy(
            src_ref=src,
            dst_ref=dst,
            send_sem=send.at[which],
            recv_sem=recv.at[which],
            device_id=device,
            device_id_type=MESH,
        )

    def landed(block, which):
        pltpu.make_async_copy(block, block, recv.at[which]).wait()

    def sent(block, which):
        pltpu.make_async_copy(block, block, send.at[which]).wait()

    def columns(there):
        return jac.at[:, pl.ds(pl.multiple_of(there * width, width), width)]

    barrier = pltpu.get_barrier_semaphore()

    def greet(device):
        pl.semaphore_signal(barrier, inc=1, device_id=device, device_id_type=MESH)

    samp_peers(lambda there: greet((there, p)))
    each(par - 1, lambda k: greet((s, lax.rem(p + 1 + k, par))))

    own = pltpu.make_async_copy(columns(s), jbuf.at[s], recv.at[0])
    own.start()
    lane = lax.broadcasted_iota(jnp.int32, (1, LANES), 1)
    offset = lax.rem(s * rows, LANES)
    mine = jnp.zeros((1, LANES), jnp.float32)
    for r in range(rows):
        mine = jnp.where(lane == offset + r, energies[r], mine)
    eown[...] = mine
    ebuf[s] = mine

    pl.semaphore_wait(barrier, samp - 1 + par - 1)

    samp_peers(lambda there: remote(columns(there), jbuf.at[s], 0, (there, p)).start())
    samp_peers(lambda there: remote(eown, ebuf.at[s], 1, (there, p)).start())

    landed(jbuf, 0)
    block = jbuf[...].reshape(count, width)
    mean_col = total_rows(block) / count
    scaled = ((block - mean_col) * (1.0 / P_SIZE**0.5)).astype(jnp.bfloat16)
    scaled_ref[...] = scaled
    part = lax.dot_general(
        scaled, scaled, (((1,), (1,)), ((), ())), preferred_element_type=jnp.float32
    )
    gpart[...] = part.reshape(gpart.shape)

    def scatter(k):
        there_y, there_x = plane_chip(k)
        there = there_y * xs + there_x
        remote(gpart.at[there], rs.at[rank], 2, on_chip(there_y, there_x, 0)).start()
        remote(
            gpart.at[chips + there, :, right],
            rs.at[rank, :, right],
            2,
            on_chip(there_y, there_x, 1),
        ).start()

    each(chips - 1, scatter)

    @pl.when(core == 0)
    def _():
        remote(gpart.at[chips + chip, :, right], rs.at[rank, :, right], 2, on_chip(y, x, 1)).start()

    @pl.when(core == 1)
    def _():
        remote(gpart.at[chip], rs.at[rank], 2, on_chip(y, x, 0)).start()

    rs[rank] = gpart[rank]

    landed(ebuf.at[pl.ds(0, samp - 1)], 1)
    level = jnp.concatenate(
        [jnp.sum(ebuf[i * per : (i + 1) * per], axis=0) for i in range(samp // per)], axis=1
    )
    right_row = total_lanes(level) / count - level
    diagonal = lax.broadcasted_iota(jnp.int32, (count, count), 0) == lax.broadcasted_iota(
        jnp.int32, (count, count), 1
    )
    right_col = total_lanes(jnp.where(diagonal, right_row, 0.0))

    others = pl.ds(0, 2 * chips - 1)
    z_others = pl.ds(0, depth - 1)

    def reduce_rows(part_of, mine_of, which):
        landed(rs.at[others, :, part_of], 2)
        ar[z, :, part_of] = jnp.sum(rs[:, :, part_of], axis=0)
        for k in z_steps[:-1]:
            remote(
                ar.at[z, :, part_of],
                ar.at[z, :, part_of],
                3,
                (samp_at(lax.rem(z + k, depth), 0, 0), p),
            ).start()
        landed(ar.at[z_others, :, part_of], 3)
        mine_of[chip] = jnp.sum(ar[:, :, part_of], axis=0)

        def spread(k):
            there_y, there_x = plane_chip(k)
            for there_core in range(CORES):
                remote(
                    mine_of.at[chip], mine_of.at[chip], which, on_chip(there_y, there_x, there_core)
                ).start()

        each(chips - 1, spread)
        remote(mine_of.at[chip], mine_of.at[chip], which, on_chip(y, x, 1 - core)).start()

    @pl.when(core == 0)
    def _():
        reduce_rows(pl.ds(0, count), top, 4)
        landed(top.at[pl.ds(0, chips - 1)], 4)
        landed(low, 5)

    @pl.when(core == 1)
    def _():
        reduce_rows(right, low, 5)
        landed(top, 4)
        landed(low.at[pl.ds(0, chips - 1)], 5)

    upper = top[...].reshape(half, count)
    lower = jnp.concatenate([jnp.transpose(upper[:, half:]), low[...].reshape(half, half)], axis=1)
    g = jnp.concatenate([upper, lower], axis=0)
    d_row, d_col = right_row, right_col
    r_row, r_col = right_row, right_col
    c_row, c_col = jnp.zeros_like(right_row), jnp.zeros_like(right_col)
    rr = total_lanes(r_row * r_row)
    for turn in range(ITERS):
        image_row = total_rows(g * d_col) + SHIFT * d_row
        size = rr / total_lanes(d_row * image_row)
        c_row = c_row + size * d_row
        c_col = c_col + size * d_col
        if turn == ITERS - 1:
            break
        image_col = total_lanes(g * d_row) + SHIFT * d_col
        r_row = r_row - size * image_row
        r_col = r_col - size * image_col
        fresh = total_lanes(r_row * r_row)
        ratio = fresh / rr
        d_row = r_row + ratio * d_row
        d_col = r_col + ratio * d_col
        rr = fresh

    upiece[s] = total_rows(scaled_ref[...].astype(jnp.float32) * c_col)
    samp_peers(lambda there: remote(upiece.at[s], upiece.at[s], 6, (there, p)).start())

    here = s // per
    piece = c_row[:, :LANES]
    for i in range(1, samp // per):
        piece = jnp.where(here == i, c_row[:, i * LANES : (i + 1) * LANES], piece)
    out[samp] = jnp.concatenate(
        [pltpu.roll(piece, lax.rem(LANES - offset, LANES), 1)] * (width // LANES), axis=1
    )

    sent(jbuf.at[pl.ds(0, samp - 1)], 0)
    sent(ebuf.at[pl.ds(0, samp - 1)], 1)

    @pl.when(core == 0)
    def _():
        sent(gpart.at[pl.ds(0, chips - 1)], 2)
        sent(gpart.at[pl.ds(0, chips), :, right], 2)
        sent(ar.at[z_others], 3)
        sent(rs.at[others], 4)

    @pl.when(core == 1)
    def _():
        sent(gpart.at[pl.ds(0, chips)], 2)
        sent(gpart.at[pl.ds(0, chips - 1), :, right], 2)
        sent(ar.at[z_others, :, right], 3)
        sent(rs.at[others, :, right], 5)

    landed(upiece.at[pl.ds(0, samp - 1)], 6)
    out[0:samp] = upiece[...]
    sent(upiece.at[pl.ds(0, samp - 1)], 6)


def solution(mesh):
    samp, par = mesh.shape["samp"], mesh.shape["par"]
    chips = Y_HI * par
    depth = samp // (CORES * Y_HI)

    def per_device(jacobian, energies):
        rows, columns = jacobian.shape
        width = columns // samp
        count = rows * samp
        half = count // 2
        share = half // chips
        out = pl.pallas_call(
            functools.partial(kernel, samp, par),
            out_shape=jax.ShapeDtypeStruct((samp + 1, 1, width), jnp.float32),
            in_specs=[
                pl.BlockSpec(memory_space=pl.ANY),
                pl.BlockSpec(memory_space=pltpu.SMEM),
            ],
            out_specs=pl.BlockSpec(memory_space=pltpu.VMEM),
            scratch_shapes=[
                pltpu.VMEM((samp, rows, width), jnp.float32),
                pltpu.VMEM((samp, 1, LANES), jnp.float32),
                pltpu.VMEM((1, LANES), jnp.float32),
                pltpu.VMEM((count, width), jnp.bfloat16),
                pltpu.VMEM((2 * chips, share, count), jnp.float32),
                pltpu.VMEM((2 * chips, share, count), jnp.float32),
                pltpu.VMEM((depth, share, count), jnp.float32),
                pltpu.VMEM((chips, share, count), jnp.float32),
                pltpu.VMEM((chips, share, half), jnp.float32),
                pltpu.VMEM((samp, 1, width), jnp.float32),
                pltpu.SemaphoreType.DMA((7,)),
                pltpu.SemaphoreType.DMA((7,)),
            ],
            compiler_params=pltpu.CompilerParams(
                collective_id=0, has_side_effects=True, vmem_limit_bytes=VMEM_BYTES
            ),
        )(
            pltpu.with_memory_space_constraint(jacobian, pltpu.HBM),
            pltpu.with_memory_space_constraint(energies, pltpu.HBM),
        )
        return out[:samp].reshape(columns), out[samp, 0, :rows]

    return jax.shard_map(
        per_device,
        mesh=mesh,
        in_specs=(P("samp", "par"), P("samp")),
        out_specs=(P("par"), P("samp")),
        check_vma=False,
    )
```

```python
import functools

import jax
import jax.numpy as jnp
from jax import lax
from jax.experimental import pallas as pl
from jax.experimental.pallas import tpu as pltpu
from jax.sharding import PartitionSpec as P

P_SIZE = 65536
ITERS = 3
SHIFT = 0.05
CORES = 2
Y_HI = 2
Y_LO = 2
LANES = 128
VMEM_BYTES = 8 * 2**20
MESH = pl.DeviceIdType.MESH


def total_rows(block):
    return jnp.sum(block, axis=0, keepdims=True)


def total_lanes(block):
    return jnp.sum(block, axis=1, keepdims=True)


def each(count, body):
    def step(k, carry):
        body(k)
        return carry

    lax.fori_loop(0, count, step, 0)


def kernel(
    samp,
    par,
    jac,
    energies,
    update,
    coeffs,
    jown,
    elist,
    jbuf,
    ebuf,
    eown,
    scaled_ref,
    gpart,
    rs,
    ar,
    top,
    low,
    upiece,
    send,
    recv,
    local,
):
    depth = samp // (CORES * Y_HI)
    xs = par // Y_LO
    ys = Y_HI * Y_LO
    chips = xs * ys
    rows, width = jbuf.shape[1], jbuf.shape[2]
    count = samp * rows
    half = count // 2
    per = LANES // rows

    s = lax.axis_index("samp")
    p = lax.axis_index("par")
    core = lax.rem(s, CORES)
    z = lax.rem(s // CORES, depth)
    y_hi = s // (CORES * depth)
    x = lax.rem(p, xs)
    y = y_hi * Y_LO + p // xs
    chip = y * xs + x
    rank = core * chips + chip
    right = pl.ds(half, half)

    def samp_at(there_z, y_off, core_off):
        there_y = lax.rem(y_hi + y_off, Y_HI)
        return (there_y * depth + there_z) * CORES + lax.rem(core + core_off, CORES)

    z_steps = sorted(range(depth), key=lambda k: -min(k, depth - k))

    def samp_peers(body):
        for z_off in z_steps:
            there_z = lax.rem(z + z_off, depth)

            def step(k):
                body(samp_at(there_z, lax.rem(k // CORES + 1, Y_HI), k + 1))

            each(CORES * Y_HI - (1 if z_off == 0 else 0), step)

    def ring(n):
        return lax.rem(2 + n * (7 - n) // 2, 4)

    def plane_chip(k):
        there_y = lax.rem(y + ring(k // xs), ys)
        return there_y, lax.rem(x + ring(lax.rem(k, xs)), xs)

    def on_chip(there_y, there_x, there_core):
        there_s = ((there_y // Y_LO) * depth + z) * CORES + there_core
        return there_s, lax.rem(there_y, Y_LO) * xs + there_x

    def remote(src, dst, which, device):
        return pltpu.make_async_remote_copy(
            src_ref=src,
            dst_ref=dst,
            send_sem=send.at[which],
            recv_sem=recv.at[which],
            device_id=device,
            device_id_type=MESH,
        )

    def landed(block, which):
        pltpu.make_async_copy(block, block, recv.at[which]).wait()

    def sent(block, which):
        pltpu.make_async_copy(block, block, send.at[which]).wait()

    def columns(there):
        return jac.at[:, pl.ds(pl.multiple_of(there * width, width), width)]

    barrier = pltpu.get_barrier_semaphore()

    def greet(device):
        pl.semaphore_signal(barrier, inc=1, device_id=device, device_id_type=MESH)

    samp_peers(lambda there: greet((there, p)))
    each(par - 1, lambda k: greet((s, lax.rem(p + 1 + k, par))))

    def stage(there):
        pltpu.make_async_copy(columns(there), jown.at[there], local.at[0]).start()

    each(samp, stage)
    level_copy = pltpu.make_async_copy(energies, elist, local.at[1])
    level_copy.start()
    level_copy.wait()
    lane = lax.broadcasted_iota(jnp.int32, (1, LANES), 1)
    offset = lax.rem(s * rows, LANES)
    mine = jnp.zeros((1, LANES), jnp.float32)
    for r in range(rows):
        mine = jnp.where(lane == offset + r, elist[r], mine)
    eown[...] = mine
    ebuf[s] = mine
    pltpu.make_async_copy(jown, jown, local.at[0]).wait()
    jbuf[s] = jown[s]

    pl.semaphore_wait(barrier, samp - 1 + par - 1)

    samp_peers(lambda there: remote(jown.at[there], jbuf.at[s], 0, (there, p)).start())
    landed(jbuf.at[pl.ds(0, samp - 1)], 0)
    block = jbuf[...].reshape(count, width)
    mean_col = total_rows(block) / count
    scaled = ((block - mean_col) * (1.0 / P_SIZE**0.5)).astype(jnp.bfloat16)
    scaled_ref[...] = scaled
    part = lax.dot_general(
        scaled, scaled, (((1,), (1,)), ((), ())), preferred_element_type=jnp.float32
    )
    gpart[...] = part.reshape(gpart.shape)

    def scatter(k):
        there_y, there_x = plane_chip(k)
        there = there_y * xs + there_x
        remote(gpart.at[there], rs.at[rank], 2, on_chip(there_y, there_x, 0)).start()
        remote(
            gpart.at[chips + there, :, right],
            rs.at[rank, :, right],
            2,
            on_chip(there_y, there_x, 1),
        ).start()

    each(chips - 1, scatter)

    @pl.when(core == 0)
    def _():
        remote(gpart.at[chips + chip, :, right], rs.at[rank, :, right], 2, on_chip(y, x, 1)).start()

    @pl.when(core == 1)
    def _():
        remote(gpart.at[chip], rs.at[rank], 2, on_chip(y, x, 0)).start()

    rs[rank] = gpart[rank]

    samp_peers(lambda there: remote(eown, ebuf.at[s], 1, (there, p)).start())

    others = pl.ds(0, 2 * chips - 1)
    z_others = pl.ds(0, depth - 1)

    every = pl.ds(0, count)

    def across_z(part_of):
        landed(rs.at[others, :, part_of], 2)
        ar[z, :, part_of] = jnp.sum(rs[:, :, part_of], axis=0)
        for k in z_steps[:-1]:
            remote(
                ar.at[z, :, part_of],
                ar.at[z, :, part_of],
                3,
                (samp_at(lax.rem(z + k, depth), 0, 0), p),
            ).start()

    def spread(part_of, mine_of, which):
        landed(ar.at[z_others, :, part_of], 3)
        mine_of[chip] = jnp.sum(ar[:, :, part_of], axis=0)

        def step(k):
            there_y, there_x = plane_chip(k)
            for there_core in range(CORES):
                remote(
                    mine_of.at[chip], mine_of.at[chip], which, on_chip(there_y, there_x, there_core)
                ).start()

        each(chips - 1, step)
        remote(mine_of.at[chip], mine_of.at[chip], which, on_chip(y, x, 1 - core)).start()

    @pl.when(core == 0)
    def _():
        across_z(every)

    @pl.when(core == 1)
    def _():
        across_z(right)

    landed(ebuf.at[pl.ds(0, samp - 1)], 1)
    level = jnp.concatenate(
        [jnp.sum(ebuf[i * per : (i + 1) * per], axis=0) for i in range(samp // per)], axis=1
    )
    right_row = total_lanes(level) / count - level
    diagonal = lax.broadcasted_iota(jnp.int32, (count, count), 0) == lax.broadcasted_iota(
        jnp.int32, (count, count), 1
    )
    right_col = total_lanes(jnp.where(diagonal, right_row, 0.0))

    @pl.when(core == 0)
    def _():
        spread(every, top, 4)
        landed(top.at[pl.ds(0, chips - 1)], 4)
        landed(low, 5)

    @pl.when(core == 1)
    def _():
        spread(right, low, 5)
        landed(top, 4)
        landed(low.at[pl.ds(0, chips - 1)], 5)

    upper = top[...].reshape(half, count)
    lower = jnp.concatenate([jnp.transpose(upper[:, half:]), low[...].reshape(half, half)], axis=1)
    g = jnp.concatenate([upper, lower], axis=0)
    d_row, d_col = right_row, right_col
    r_row, r_col = right_row, right_col
    c_row, c_col = jnp.zeros_like(right_row), jnp.zeros_like(right_col)
    rr = total_lanes(r_row * r_row)
    for turn in range(ITERS):
        image_row = total_rows(g * d_col) + SHIFT * d_row
        size = rr / total_lanes(d_row * image_row)
        c_row = c_row + size * d_row
        c_col = c_col + size * d_col
        if turn == ITERS - 1:
            break
        image_col = total_lanes(g * d_row) + SHIFT * d_col
        r_row = r_row - size * image_row
        r_col = r_col - size * image_col
        fresh = total_lanes(r_row * r_row)
        ratio = fresh / rr
        d_row = r_row + ratio * d_row
        d_col = r_col + ratio * d_col
        rr = fresh

    upiece[s] = total_rows(scaled_ref[...].astype(jnp.float32) * c_col)
    samp_peers(lambda there: remote(upiece.at[s], upiece.at[s], 6, (there, p)).start())

    here = s // per
    piece = c_row[:, :LANES]
    for i in range(1, samp // per):
        piece = jnp.where(here == i, c_row[:, i * LANES : (i + 1) * LANES], piece)
    coeffs[...] = pltpu.roll(piece, lax.rem(LANES - offset, LANES), 1)[0, :rows]

    sent(jbuf.at[pl.ds(0, samp - 1)], 0)
    sent(ebuf.at[pl.ds(0, samp - 1)], 1)

    @pl.when(core == 0)
    def _():
        sent(gpart.at[pl.ds(0, chips - 1)], 2)
        sent(gpart.at[pl.ds(0, chips), :, right], 2)
        sent(ar.at[z_others], 3)
        sent(rs.at[others], 4)

    @pl.when(core == 1)
    def _():
        sent(gpart.at[pl.ds(0, chips)], 2)
        sent(gpart.at[pl.ds(0, chips - 1), :, right], 2)
        sent(ar.at[z_others, :, right], 3)
        sent(rs.at[others, :, right], 5)

    landed(upiece.at[pl.ds(0, samp - 1)], 6)
    update[...] = upiece[...]
    sent(upiece.at[pl.ds(0, samp - 1)], 6)


def hand_over_kernel(update, coeffs, update_out, coeffs_out, done):
    first = pltpu.make_async_copy(update, update_out, done.at[0])
    second = pltpu.make_async_copy(coeffs, coeffs_out, done.at[1])
    first.start()
    second.start()
    first.wait()
    second.wait()


def hand_over(update, coeffs):
    anywhere = pl.BlockSpec(memory_space=pl.ANY)
    return pl.pallas_call(
        hand_over_kernel,
        out_shape=(
            jax.ShapeDtypeStruct(update.shape, update.dtype),
            jax.ShapeDtypeStruct(coeffs.shape, coeffs.dtype),
        ),
        in_specs=[anywhere, anywhere],
        out_specs=(anywhere, anywhere),
        scratch_shapes=[pltpu.SemaphoreType.DMA((2,))],
        compiler_params=pltpu.CompilerParams(vmem_limit_bytes=VMEM_BYTES),
    )(update, coeffs)


def solution(mesh):
    samp, par = mesh.shape["samp"], mesh.shape["par"]
    chips = Y_HI * par
    depth = samp // (CORES * Y_HI)

    def per_device(jacobian, energies):
        rows, columns = jacobian.shape
        width = columns // samp
        count = rows * samp
        half = count // 2
        share = half // chips
        update, coeffs = pl.pallas_call(
            functools.partial(kernel, samp, par),
            out_shape=(
                jax.ShapeDtypeStruct((samp, 1, width), jnp.float32),
                jax.ShapeDtypeStruct((rows,), jnp.float32),
            ),
            in_specs=[
                pl.BlockSpec(memory_space=pl.ANY),
                pl.BlockSpec(memory_space=pl.ANY),
            ],
            out_specs=(
                pl.BlockSpec(memory_space=pltpu.VMEM),
                pl.BlockSpec(memory_space=pltpu.VMEM),
            ),
            scratch_shapes=[
                pltpu.VMEM((samp, rows, width), jnp.float32),
                pltpu.SMEM((rows,), jnp.float32),
                pltpu.VMEM((samp, rows, width), jnp.float32),
                pltpu.VMEM((samp, 1, LANES), jnp.float32),
                pltpu.VMEM((1, LANES), jnp.float32),
                pltpu.VMEM((count, width), jnp.bfloat16),
                pltpu.VMEM((2 * chips, share, count), jnp.float32),
                pltpu.VMEM((2 * chips, share, count), jnp.float32),
                pltpu.VMEM((depth, share, count), jnp.float32),
                pltpu.VMEM((chips, share, count), jnp.float32),
                pltpu.VMEM((chips, share, half), jnp.float32),
                pltpu.VMEM((samp, 1, width), jnp.float32),
                pltpu.SemaphoreType.DMA((7,)),
                pltpu.SemaphoreType.DMA((7,)),
                pltpu.SemaphoreType.DMA((2,)),
            ],
            compiler_params=pltpu.CompilerParams(
                collective_id=0, has_side_effects=True, vmem_limit_bytes=VMEM_BYTES
            ),
        )(
            pltpu.with_memory_space_constraint(jacobian, pltpu.HBM),
            pltpu.with_memory_space_constraint(energies, pltpu.HBM),
        )
        return hand_over(update.reshape(columns), coeffs)

    return jax.shard_map(
        per_device,
        mesh=mesh,
        in_specs=(P("samp", "par"), P("samp")),
        out_specs=(P("par"), P("samp")),
        check_vma=False,
    )
```

```python
import functools

import jax
import jax.numpy as jnp
from jax import lax
from jax.experimental import pallas as pl
from jax.experimental.pallas import tpu as pltpu
from jax.sharding import PartitionSpec as P

P_SIZE = 65536
ITERS = 3
SHIFT = 0.05
CORES = 2
Y_HI = 2
Y_LO = 2
LANES = 128
VMEM_BYTES = 8 * 2**20
MESH = pl.DeviceIdType.MESH


def total_rows(block):
    return jnp.sum(block, axis=0, keepdims=True)


def total_lanes(block):
    return jnp.sum(block, axis=1, keepdims=True)


def each(count, body):
    def step(k, carry):
        body(k)
        return carry

    lax.fori_loop(0, count, step, 0)


def kernel(
    samp,
    par,
    jac,
    energies,
    update,
    coeffs,
    jown,
    elist,
    jbuf,
    ebuf,
    eown,
    scaled_ref,
    gpart,
    rs,
    ar,
    top,
    low,
    send,
    recv,
    local,
):
    depth = samp // (CORES * Y_HI)
    xs = par // Y_LO
    ys = Y_HI * Y_LO
    chips = xs * ys
    rows, width = jbuf.shape[1], jbuf.shape[2]
    count = samp * rows
    half = count // 2
    per = LANES // rows

    s = lax.axis_index("samp")
    p = lax.axis_index("par")
    core = lax.rem(s, CORES)
    z = lax.rem(s // CORES, depth)
    y_hi = s // (CORES * depth)
    x = lax.rem(p, xs)
    y = y_hi * Y_LO + p // xs
    chip = y * xs + x
    rank = core * chips + chip
    right = pl.ds(half, half)

    def away(step, size):
        return min(step, size - step)

    y_at = [lax.rem(y + k, ys) for k in range(ys)]
    x_at = [lax.rem(x + k, xs) for k in range(xs)]
    z_at = [lax.rem(z + k, depth) for k in range(depth)]
    y_hi_at = [lax.rem(y_hi + k, Y_HI) for k in range(Y_HI)]
    core_at = [core, 1 - core]
    plane_s = [((there // Y_LO) * depth + z) * CORES for there in y_at]
    plane_p = [lax.rem(there, Y_LO) * xs for there in y_at]
    z_steps = sorted(range(1, depth), key=lambda k: -away(k, depth))
    chip_steps = sorted(
        [(j, i) for j in range(ys) for i in range(xs) if (j, i) != (0, 0)],
        key=lambda k: -away(k[0], ys) - away(k[1], xs),
    )
    samp_steps = sorted(
        [(j, k, c) for j in range(Y_HI) for k in range(depth) for c in range(CORES) if j + k + c],
        key=lambda k: (-2 * k[0] - away(k[1], depth), -k[2]),
    )
    samp_ids = [(y_hi_at[j] * depth + z_at[k]) * CORES + core_at[c] for j, k, c in samp_steps]
    z_ids = [(y_hi * depth + z_at[k]) * CORES + core for k in z_steps]

    def samp_peers(body):
        for there in samp_ids:
            body(there)

    def on_chip(step, there_core):
        return plane_s[step[0]] + there_core, plane_p[step[0]] + x_at[step[1]]

    def chip_of(step):
        return y_at[step[0]] * xs + x_at[step[1]]

    here_chip = (0, 0)

    def remote(src, dst, which, device):
        return pltpu.make_async_remote_copy(
            src_ref=src,
            dst_ref=dst,
            send_sem=send.at[which],
            recv_sem=recv.at[which],
            device_id=device,
            device_id_type=MESH,
        )

    def landed(block, which):
        pltpu.make_async_copy(block, block, recv.at[which]).wait()

    def sent(block, which):
        pltpu.make_async_copy(block, block, send.at[which]).wait()

    def columns(there):
        return jac.at[:, pl.ds(pl.multiple_of(there * width, width), width)]

    barrier = pltpu.get_barrier_semaphore()

    def greet(device):
        pl.semaphore_signal(barrier, inc=1, device_id=device, device_id_type=MESH)

    samp_peers(lambda there: greet((there, p)))
    each(par - 1, lambda k: greet((s, lax.rem(p + 1 + k, par))))

    def stage(there):
        pltpu.make_async_copy(columns(there), jown.at[there], local.at[0]).start()

    each(samp, stage)
    level_copy = pltpu.make_async_copy(energies, elist, local.at[1])
    level_copy.start()
    level_copy.wait()
    lane = lax.broadcasted_iota(jnp.int32, (1, LANES), 1)
    offset = lax.rem(s * rows, LANES)
    mine = jnp.zeros((1, LANES), jnp.float32)
    for r in range(rows):
        mine = jnp.where(lane == offset + r, elist[r], mine)
    eown[...] = mine
    ebuf[s] = mine
    pltpu.make_async_copy(jown, jown, local.at[0]).wait()
    jbuf[s] = jown[s]

    pl.semaphore_wait(barrier, samp - 1 + par - 1)

    samp_peers(lambda there: remote(jown.at[there], jbuf.at[s], 0, (there, p)).start())
    landed(jbuf.at[pl.ds(0, samp - 1)], 0)
    block = jbuf[...].reshape(count, width)
    mean_col = total_rows(block) / count
    scaled = ((block - mean_col) * (1.0 / P_SIZE**0.5)).astype(jnp.bfloat16)
    scaled_ref[...] = scaled
    part = lax.dot_general(
        scaled, scaled, (((1,), (1,)), ((), ())), preferred_element_type=jnp.float32
    )
    gpart[...] = part.reshape(gpart.shape)

    def scatter(k):
        there = chip_of(k)
        remote(gpart.at[there], rs.at[rank], 2, on_chip(k, 0)).start()
        remote(
            gpart.at[chips + there, :, right],
            rs.at[rank, :, right],
            2,
            on_chip(k, 1),
        ).start()

    for k in chip_steps:
        scatter(k)

    @pl.when(core == 0)
    def _():
        remote(gpart.at[chips + chip, :, right], rs.at[rank, :, right], 2, on_chip(here_chip, 1)).start()

    @pl.when(core == 1)
    def _():
        remote(gpart.at[chip], rs.at[rank], 2, on_chip(here_chip, 0)).start()

    rs[rank] = gpart[rank]

    samp_peers(lambda there: remote(eown, ebuf.at[s], 1, (there, p)).start())

    others = pl.ds(0, 2 * chips - 1)
    z_others = pl.ds(0, depth - 1)

    every = pl.ds(0, count)

    def across_z(part_of):
        landed(rs.at[others, :, part_of], 2)
        ar[z, :, part_of] = jnp.sum(rs[:, :, part_of], axis=0)
        for there in z_ids:
            remote(
                ar.at[z, :, part_of],
                ar.at[z, :, part_of],
                3,
                (there, p),
            ).start()

    def spread(part_of, mine_of, which):
        landed(ar.at[z_others, :, part_of], 3)
        mine_of[chip] = jnp.sum(ar[:, :, part_of], axis=0)

        def step(k):
            for there_core in range(CORES):
                remote(
                    mine_of.at[chip], mine_of.at[chip], which, on_chip(k, there_core)
                ).start()

        for k in chip_steps:
            step(k)
        remote(mine_of.at[chip], mine_of.at[chip], which, on_chip(here_chip, 1 - core)).start()

    @pl.when(core == 0)
    def _():
        across_z(every)

    @pl.when(core == 1)
    def _():
        across_z(right)

    landed(ebuf.at[pl.ds(0, samp - 1)], 1)
    level = jnp.concatenate(
        [jnp.sum(ebuf[i * per : (i + 1) * per], axis=0) for i in range(samp // per)], axis=1
    )
    right_row = total_lanes(level) / count - level
    diagonal = lax.broadcasted_iota(jnp.int32, (count, count), 0) == lax.broadcasted_iota(
        jnp.int32, (count, count), 1
    )
    right_col = total_lanes(jnp.where(diagonal, right_row, 0.0))

    @pl.when(core == 0)
    def _():
        spread(every, top, 4)
        landed(top.at[pl.ds(0, chips - 1)], 4)
        landed(low, 5)

    @pl.when(core == 1)
    def _():
        spread(right, low, 5)
        landed(top, 4)
        landed(low.at[pl.ds(0, chips - 1)], 5)

    upper = top[...].reshape(half, count)
    lower = jnp.concatenate([jnp.transpose(upper[:, half:]), low[...].reshape(half, half)], axis=1)
    g = jnp.concatenate([upper, lower], axis=0)
    d_row, d_col = right_row, right_col
    r_row, r_col = right_row, right_col
    c_row, c_col = jnp.zeros_like(right_row), jnp.zeros_like(right_col)
    rr = total_lanes(r_row * r_row)
    for turn in range(ITERS):
        image_row = total_rows(g * d_col) + SHIFT * d_row
        size = rr / total_lanes(d_row * image_row)
        c_row = c_row + size * d_row
        c_col = c_col + size * d_col
        if turn == ITERS - 1:
            break
        image_col = total_lanes(g * d_row) + SHIFT * d_col
        r_row = r_row - size * image_row
        r_col = r_col - size * image_col
        fresh = total_lanes(r_row * r_row)
        ratio = fresh / rr
        d_row = r_row + ratio * d_row
        d_col = r_col + ratio * d_col
        rr = fresh

    update[s] = total_rows(scaled_ref[...].astype(jnp.float32) * c_col)
    samp_peers(lambda there: remote(update.at[s], update.at[s], 6, (there, p)).start())

    here = s // per
    piece = c_row[:, :LANES]
    for i in range(1, samp // per):
        piece = jnp.where(here == i, c_row[:, i * LANES : (i + 1) * LANES], piece)
    coeffs[...] = pltpu.roll(piece, lax.rem(LANES - offset, LANES), 1)[0, :rows]

    sent(jbuf.at[pl.ds(0, samp - 1)], 0)
    sent(ebuf.at[pl.ds(0, samp - 1)], 1)

    @pl.when(core == 0)
    def _():
        sent(gpart.at[pl.ds(0, chips - 1)], 2)
        sent(gpart.at[pl.ds(0, chips), :, right], 2)
        sent(ar.at[z_others], 3)
        sent(rs.at[others], 4)

    @pl.when(core == 1)
    def _():
        sent(gpart.at[pl.ds(0, chips)], 2)
        sent(gpart.at[pl.ds(0, chips - 1), :, right], 2)
        sent(ar.at[z_others, :, right], 3)
        sent(rs.at[others, :, right], 5)

    sent(update.at[pl.ds(0, samp - 1)], 6)
    landed(update.at[pl.ds(0, samp - 1)], 6)


def hand_over_kernel(update, coeffs, update_out, coeffs_out, done):
    first = pltpu.make_async_copy(update, update_out, done.at[0])
    second = pltpu.make_async_copy(coeffs, coeffs_out, done.at[1])
    first.start()
    second.start()
    first.wait()
    second.wait()


def hand_over(update, coeffs):
    anywhere = pl.BlockSpec(memory_space=pl.ANY)
    return pl.pallas_call(
        hand_over_kernel,
        out_shape=(
            jax.ShapeDtypeStruct(update.shape, update.dtype),
            jax.ShapeDtypeStruct(coeffs.shape, coeffs.dtype),
        ),
        in_specs=[anywhere, anywhere],
        out_specs=(anywhere, anywhere),
        scratch_shapes=[pltpu.SemaphoreType.DMA((2,))],
        compiler_params=pltpu.CompilerParams(vmem_limit_bytes=VMEM_BYTES),
    )(update, coeffs)


def solution(mesh):
    samp, par = mesh.shape["samp"], mesh.shape["par"]
    chips = Y_HI * par
    depth = samp // (CORES * Y_HI)

    def per_device(jacobian, energies):
        rows, columns = jacobian.shape
        width = columns // samp
        count = rows * samp
        half = count // 2
        share = half // chips
        update, coeffs = pl.pallas_call(
            functools.partial(kernel, samp, par),
            out_shape=(
                jax.ShapeDtypeStruct((samp, 1, width), jnp.float32),
                jax.ShapeDtypeStruct((rows,), jnp.float32),
            ),
            in_specs=[
                pl.BlockSpec(memory_space=pl.ANY),
                pl.BlockSpec(memory_space=pl.ANY),
            ],
            out_specs=(
                pl.BlockSpec(memory_space=pltpu.VMEM),
                pl.BlockSpec(memory_space=pltpu.VMEM),
            ),
            scratch_shapes=[
                pltpu.VMEM((samp, rows, width), jnp.float32),
                pltpu.SMEM((rows,), jnp.float32),
                pltpu.VMEM((samp, rows, width), jnp.float32),
                pltpu.VMEM((samp, 1, LANES), jnp.float32),
                pltpu.VMEM((1, LANES), jnp.float32),
                pltpu.VMEM((count, width), jnp.bfloat16),
                pltpu.VMEM((2 * chips, share, count), jnp.float32),
                pltpu.VMEM((2 * chips, share, count), jnp.float32),
                pltpu.VMEM((depth, share, count), jnp.float32),
                pltpu.VMEM((chips, share, count), jnp.float32),
                pltpu.VMEM((chips, share, half), jnp.float32),
                pltpu.SemaphoreType.DMA((7,)),
                pltpu.SemaphoreType.DMA((7,)),
                pltpu.SemaphoreType.DMA((2,)),
            ],
            compiler_params=pltpu.CompilerParams(
                collective_id=0, has_side_effects=True, vmem_limit_bytes=VMEM_BYTES
            ),
        )(
            pltpu.with_memory_space_constraint(jacobian, pltpu.HBM),
            pltpu.with_memory_space_constraint(energies, pltpu.HBM),
        )
        return hand_over(update.reshape(columns), coeffs)

    return jax.shard_map(
        per_device,
        mesh=mesh,
        in_specs=(P("samp", "par"), P("samp")),
        out_specs=(P("par"), P("samp")),
        check_vma=False,
    )
```

```python
import functools

import jax
import jax.numpy as jnp
from jax import lax
from jax.experimental import pallas as pl
from jax.experimental.pallas import tpu as pltpu
from jax.sharding import PartitionSpec as P

P_SIZE = 65536
ITERS = 3
SHIFT = 0.05
CORES = 2
Y_HI = 2
Y_LO = 2
LANES = 128
VMEM_BYTES = 8 * 2**20
MESH = pl.DeviceIdType.MESH


def total_rows(block):
    return jnp.sum(block, axis=0, keepdims=True)


def total_lanes(block):
    return jnp.sum(block, axis=1, keepdims=True)


def each(count, body):
    def step(k, carry):
        body(k)
        return carry

    lax.fori_loop(0, count, step, 0)


def kernel(
    samp,
    par,
    jac,
    energies,
    update,
    coeffs,
    jown,
    elist,
    jbuf,
    ebuf,
    eown,
    scaled_ref,
    gpart,
    rs,
    ar,
    top,
    low,
    cown,
    cbuf,
    send,
    recv,
    local,
):
    depth = samp // (CORES * Y_HI)
    team = samp // Y_HI
    xs = par // Y_LO
    chips = par
    rows, width = jbuf.shape[1], jbuf.shape[2]
    count = samp * rows
    half = count // 2
    per = LANES // rows

    s = lax.axis_index("samp")
    p = lax.axis_index("par")
    core = lax.rem(s, CORES)
    z = lax.rem(s // CORES, depth)
    x = lax.rem(p, xs)
    y = p // xs
    rank = core * chips + p
    right = pl.ds(half, half)
    worker = s < team
    sender = jnp.logical_not(worker)

    def away(step, size):
        return min(step, size - step)

    x_at = [lax.rem(x + k, xs) for k in range(xs)]
    y_at = [y, 1 - y]
    z_at = [lax.rem(z + k, depth) for k in range(depth)]
    core_at = [core, 1 - core]
    z_steps = sorted(range(depth), key=lambda k: -away(k, depth))
    z_ids = [z_at[k] * CORES + core for k in z_steps[:-1]]
    team_ids = [z_at[k] * CORES + core_at[c] for k in z_steps for c in (1, 0)]
    chip_steps = sorted(
        [(j, i) for j in range(Y_LO) for i in range(xs) if (j, i) != (0, 0)],
        key=lambda k: -k[0] - away(k[1], xs),
    )
    chip_ids = [y_at[j] * xs + x_at[i] for j, i in chip_steps]

    def at_core(there_core):
        return z * CORES + there_core

    def remote(src, dst, which, device):
        return pltpu.make_async_remote_copy(
            src_ref=src,
            dst_ref=dst,
            send_sem=send.at[which],
            recv_sem=recv.at[which],
            device_id=device,
            device_id_type=MESH,
        )

    def landed(block, which):
        pltpu.make_async_copy(block, block, recv.at[which]).wait()

    def sent(block, which):
        pltpu.make_async_copy(block, block, send.at[which]).wait()

    def columns(there):
        return jac.at[:, pl.ds(pl.multiple_of(there * width, width), width)]

    barrier = pltpu.get_barrier_semaphore()

    def greet(device):
        pl.semaphore_signal(barrier, inc=1, device_id=device, device_id_type=MESH)

    @pl.when(worker)
    def _():
        for there in team_ids:
            greet((there + team, p))
        for there in team_ids[:-1]:
            greet((there, p))
        each(par - 1, lambda k: greet((s, lax.rem(p + 1 + k, par))))

    def stage(there):
        pltpu.make_async_copy(columns(there), jown.at[there], local.at[0]).start()

    each(team, stage)
    level_copy = pltpu.make_async_copy(energies, elist, local.at[1])
    level_copy.start()
    level_copy.wait()
    lane = lax.broadcasted_iota(jnp.int32, (1, LANES), 1)
    offset = lax.rem(s * rows, LANES)
    mine = jnp.zeros((1, LANES), jnp.float32)
    for r in range(rows):
        mine = jnp.where(lane == offset + r, elist[r], mine)
    eown[...] = mine
    pltpu.make_async_copy(jown, jown, local.at[0]).wait()

    def give_rows(there):
        remote(jown.at[there], jbuf.at[s], 0, (there, p)).start()

    def give_energies(there):
        remote(eown, ebuf.at[s], 1, (there, p)).start()

    def work():
        block = jbuf[...].reshape(count, width)
        mean_col = total_rows(block) / count
        scaled = ((block - mean_col) * (1.0 / P_SIZE**0.5)).astype(jnp.bfloat16)
        scaled_ref[...] = scaled
        part = lax.dot_general(
            scaled, scaled, (((1,), (1,)), ((), ())), preferred_element_type=jnp.float32
        )
        gpart[...] = part.reshape(gpart.shape)

        def scatter(there):
            remote(gpart.at[there], rs.at[rank], 2, (at_core(0), there)).start()
            remote(
                gpart.at[chips + there, :, right], rs.at[rank, :, right], 2, (at_core(1), there)
            ).start()

        for there in chip_ids:
            scatter(there)

        @pl.when(core == 0)
        def _():
            remote(gpart.at[chips + p, :, right], rs.at[rank, :, right], 2, (at_core(1), p)).start()

        @pl.when(core == 1)
        def _():
            remote(gpart.at[p], rs.at[rank], 2, (at_core(0), p)).start()

        rs[rank] = gpart[rank]
        for there in team_ids[:-1]:
            give_energies(there)

        others = pl.ds(0, 2 * chips - 1)
        z_others = pl.ds(0, depth - 1)
        every = pl.ds(0, count)

        def across_z(part_of):
            landed(rs.at[others, :, part_of], 2)
            ar[z, :, part_of] = jnp.sum(rs[:, :, part_of], axis=0)
            for there in z_ids:
                remote(ar.at[z, :, part_of], ar.at[z, :, part_of], 3, (there, p)).start()

        def spread(part_of, mine_of, which):
            landed(ar.at[z_others, :, part_of], 3)
            mine_of[p] = jnp.sum(ar[:, :, part_of], axis=0)
            for there in chip_ids:
                for there_core in range(CORES):
                    remote(mine_of.at[p], mine_of.at[p], which, (at_core(there_core), there)).start()
            remote(mine_of.at[p], mine_of.at[p], which, (at_core(1 - core), p)).start()

        @pl.when(core == 0)
        def _():
            across_z(every)

        @pl.when(core == 1)
        def _():
            across_z(right)

        landed(ebuf.at[pl.ds(0, samp - 1)], 1)
        level = jnp.concatenate(
            [jnp.sum(ebuf[i * per : (i + 1) * per], axis=0) for i in range(samp // per)], axis=1
        )
        right_row = total_lanes(level) / count - level
        diagonal = lax.broadcasted_iota(jnp.int32, (count, count), 0) == lax.broadcasted_iota(
            jnp.int32, (count, count), 1
        )
        right_col = total_lanes(jnp.where(diagonal, right_row, 0.0))

        @pl.when(core == 0)
        def _():
            spread(every, top, 4)
            landed(top.at[pl.ds(0, chips - 1)], 4)
            landed(low, 5)

        @pl.when(core == 1)
        def _():
            spread(right, low, 5)
            landed(top, 4)
            landed(low.at[pl.ds(0, chips - 1)], 5)

        above = top[...].reshape(half, count)
        below = jnp.concatenate([jnp.transpose(above[:, half:]), low[...].reshape(half, half)], axis=1)
        g = jnp.concatenate([above, below], axis=0)
        d_row, d_col = right_row, right_col
        r_row, r_col = right_row, right_col
        c_row, c_col = jnp.zeros_like(right_row), jnp.zeros_like(right_col)
        rr = total_lanes(r_row * r_row)
        for turn in range(ITERS):
            image_row = total_rows(g * d_col) + SHIFT * d_row
            size = rr / total_lanes(d_row * image_row)
            c_row = c_row + size * d_row
            c_col = c_col + size * d_col
            if turn == ITERS - 1:
                break
            image_col = total_lanes(g * d_row) + SHIFT * d_col
            r_row = r_row - size * image_row
            r_col = r_col - size * image_col
            fresh = total_lanes(r_row * r_row)
            ratio = fresh / rr
            d_row = r_row + ratio * d_row
            d_col = r_col + ratio * d_col
            rr = fresh

        update[s] = total_rows(scaled_ref[...].astype(jnp.float32) * c_col)

        def give_piece(there):
            remote(update.at[s], update.at[s], 6, (there, p)).start()

        for there in team_ids[:-1]:
            give_piece(there)
            give_piece(there + team)
        give_piece(s + team)

        def own_samples(first):
            here = lax.rem(s, team) // per
            piece = c_row[:, first : first + LANES]
            for i in range(1, team // per):
                piece = jnp.where(here == i, c_row[:, first + i * LANES : first + (i + 1) * LANES], piece)
            return pltpu.roll(piece, lax.rem(LANES - offset, LANES), 1)

        cown[...] = own_samples(half)
        remote(cown, cbuf, 7, (s + team, p)).start()
        coeffs[...] = own_samples(0)[0, :rows]

        sent(jbuf.at[pl.ds(0, team - 1)], 0)
        sent(ebuf.at[pl.ds(0, team - 1)], 1)

        @pl.when(core == 0)
        def _():
            sent(gpart.at[pl.ds(0, chips - 1)], 2)
            sent(gpart.at[pl.ds(0, chips), :, right], 2)
            sent(ar.at[z_others], 3)
            sent(rs.at[others], 4)

        @pl.when(core == 1)
        def _():
            sent(gpart.at[pl.ds(0, chips)], 2)
            sent(gpart.at[pl.ds(0, chips - 1), :, right], 2)
            sent(ar.at[z_others, :, right], 3)
            sent(rs.at[others, :, right], 5)

        sent(update, 6)
        sent(update.at[pl.ds(0, team - 1)], 6)
        sent(cown, 7)
        landed(update.at[pl.ds(0, team - 1)], 6)


    @pl.when(sender)
    def _():
        pl.semaphore_wait(barrier, team)
        for there in team_ids:
            give_rows(there)
        for there in team_ids:
            give_energies(there)
        landed(cbuf, 7)
        coeffs[...] = cbuf[...][0, :rows]
        sent(jbuf.at[pl.ds(0, team)], 0)
        sent(ebuf.at[pl.ds(0, team)], 1)
        landed(update, 6)

    @pl.when(worker)
    def _():
        pl.semaphore_wait(barrier, team - 1 + par - 1)
        for there in team_ids[:-1]:
            give_rows(there)
        ebuf[s] = mine
        jbuf[s] = jown[s]
        landed(jbuf.at[pl.ds(0, samp - 1)], 0)
        work()


def hand_over_kernel(update, coeffs, update_out, coeffs_out, done):
    first = pltpu.make_async_copy(update, update_out, done.at[0])
    second = pltpu.make_async_copy(coeffs, coeffs_out, done.at[1])
    first.start()
    second.start()
    first.wait()
    second.wait()


def hand_over(update, coeffs):
    anywhere = pl.BlockSpec(memory_space=pl.ANY)
    return pl.pallas_call(
        hand_over_kernel,
        out_shape=(
            jax.ShapeDtypeStruct(update.shape, update.dtype),
            jax.ShapeDtypeStruct(coeffs.shape, coeffs.dtype),
        ),
        in_specs=[anywhere, anywhere],
        out_specs=(anywhere, anywhere),
        scratch_shapes=[pltpu.SemaphoreType.DMA((2,))],
        compiler_params=pltpu.CompilerParams(vmem_limit_bytes=VMEM_BYTES),
    )(update, coeffs)


def solution(mesh):
    samp, par = mesh.shape["samp"], mesh.shape["par"]
    chips = par
    depth = samp // (CORES * Y_HI)
    team = samp // Y_HI

    def per_device(jacobian, energies):
        rows, columns = jacobian.shape
        width = columns // team
        count = rows * samp
        half = count // 2
        share = half // chips
        update, coeffs = pl.pallas_call(
            functools.partial(kernel, samp, par),
            out_shape=(
                jax.ShapeDtypeStruct((team, 1, width), jnp.float32),
                jax.ShapeDtypeStruct((rows,), jnp.float32),
            ),
            in_specs=[
                pl.BlockSpec(memory_space=pl.ANY),
                pl.BlockSpec(memory_space=pl.ANY),
            ],
            out_specs=(
                pl.BlockSpec(memory_space=pltpu.VMEM),
                pl.BlockSpec(memory_space=pltpu.VMEM),
            ),
            scratch_shapes=[
                pltpu.VMEM((team, rows, width), jnp.float32),
                pltpu.SMEM((rows,), jnp.float32),
                pltpu.VMEM((samp, rows, width), jnp.float32),
                pltpu.VMEM((samp, 1, LANES), jnp.float32),
                pltpu.VMEM((1, LANES), jnp.float32),
                pltpu.VMEM((count, width), jnp.bfloat16),
                pltpu.VMEM((2 * chips, share, count), jnp.float32),
                pltpu.VMEM((2 * chips, share, count), jnp.float32),
                pltpu.VMEM((depth, share, count), jnp.float32),
                pltpu.VMEM((chips, share, count), jnp.float32),
                pltpu.VMEM((chips, share, half), jnp.float32),
                pltpu.VMEM((1, LANES), jnp.float32),
                pltpu.VMEM((1, LANES), jnp.float32),
                pltpu.SemaphoreType.DMA((8,)),
                pltpu.SemaphoreType.DMA((8,)),
                pltpu.SemaphoreType.DMA((2,)),
            ],
            compiler_params=pltpu.CompilerParams(
                collective_id=0, has_side_effects=True, vmem_limit_bytes=VMEM_BYTES
            ),
        )(
            pltpu.with_memory_space_constraint(jacobian, pltpu.HBM),
            pltpu.with_memory_space_constraint(energies, pltpu.HBM),
        )
        return hand_over(update.reshape(columns), coeffs)

    return jax.shard_map(
        per_device,
        mesh=mesh,
        in_specs=(P("samp", "par"), P("samp")),
        out_specs=(P("par"), P("samp")),
        check_vma=False,
    )
```

```python
import functools

import jax
import jax.numpy as jnp
from jax import lax
from jax.experimental import pallas as pl
from jax.experimental.pallas import tpu as pltpu
from jax.sharding import PartitionSpec as P

P_SIZE = 65536
ITERS = 3
SHIFT = 0.05
CORES = 2
Y_HI = 2
Y_LO = 2
LANES = 128
VMEM_BYTES = 8 * 2**20
MESH = pl.DeviceIdType.MESH


def total_rows(block):
    return jnp.sum(block, axis=0, keepdims=True)


def total_lanes(block):
    return jnp.sum(block, axis=1, keepdims=True)


def each(count, body):
    def step(k, carry):
        body(k)
        return carry

    lax.fori_loop(0, count, step, 0)


def kernel(
    samp,
    par,
    jac,
    energies,
    update,
    coeffs,
    jown,
    elist,
    jbuf,
    ebuf,
    eown,
    scaled_ref,
    gpart,
    rs,
    ar,
    top,
    low,
    cown,
    cbuf,
    send,
    recv,
    local,
):
    depth = samp // (CORES * Y_HI)
    team = samp // Y_HI
    xs = par // Y_LO
    chips = par
    rows, width = jbuf.shape[1], jbuf.shape[2]
    count = samp * rows
    half = count // 2
    per = LANES // rows

    s = lax.axis_index("samp")
    p = lax.axis_index("par")
    core = lax.rem(s, CORES)
    z = lax.rem(s // CORES, depth)
    x = lax.rem(p, xs)
    y = p // xs
    rank = core * chips + p
    right = pl.ds(half, half)
    worker = s < team
    sender = jnp.logical_not(worker)

    def away(step, size):
        return min(step, size - step)

    x_at = [lax.rem(x + k, xs) for k in range(xs)]
    y_at = [y, 1 - y]
    z_at = [lax.rem(z + k, depth) for k in range(depth)]
    core_at = [core, 1 - core]
    z_steps = sorted(range(depth), key=lambda k: -away(k, depth))
    z_ids = [z_at[k] * CORES + core for k in z_steps[:-1]]
    team_ids = [z_at[k] * CORES + core_at[c] for k in z_steps for c in (1, 0)]
    chip_steps = sorted(
        [(j, i) for j in range(Y_LO) for i in range(xs) if (j, i) != (0, 0)],
        key=lambda k: -k[0] - away(k[1], xs),
    )
    chip_ids = [y_at[j] * xs + x_at[i] for j, i in chip_steps]

    def at_core(there_core):
        return z * CORES + there_core

    def remote(src, dst, which, device):
        return pltpu.make_async_remote_copy(
            src_ref=src,
            dst_ref=dst,
            send_sem=send.at[which],
            recv_sem=recv.at[which],
            device_id=device,
            device_id_type=MESH,
        )

    def landed(block, which):
        pltpu.make_async_copy(block, block, recv.at[which]).wait()

    def sent(block, which):
        pltpu.make_async_copy(block, block, send.at[which]).wait()

    def columns(there):
        return jac.at[:, pl.ds(pl.multiple_of(there * width, width), width)]

    barrier = pltpu.get_barrier_semaphore()

    def greet(device):
        pl.semaphore_signal(barrier, inc=1, device_id=device, device_id_type=MESH)

    @pl.when(worker)
    def _():
        for there in team_ids:
            greet((there + team, p))
        for there in team_ids[:-1]:
            greet((there, p))
        each(par - 1, lambda k: greet((s, lax.rem(p + 1 + k, par))))

    def stage(there):
        pltpu.make_async_copy(columns(there), jown.at[there], local.at[0]).start()

    each(team, stage)
    level_copy = pltpu.make_async_copy(energies, elist, local.at[1])
    level_copy.start()
    level_copy.wait()
    lane = lax.broadcasted_iota(jnp.int32, (1, LANES), 1)
    offset = lax.rem(s * rows, LANES)
    mine = jnp.zeros((1, LANES), jnp.float32)
    for r in range(rows):
        mine = jnp.where(lane == offset + r, elist[r], mine)
    eown[...] = mine
    pltpu.make_async_copy(jown, jown, local.at[0]).wait()

    def give_rows(there):
        remote(jown.at[there], jbuf.at[s], 0, (there, p)).start()

    def give_energies(there):
        remote(eown, ebuf.at[s], 1, (there, p)).start()

    def work():
        block = jbuf[...].reshape(count, width)
        mean_col = total_rows(block) / count
        scaled = ((block - mean_col) * (1.0 / P_SIZE**0.5)).astype(jnp.bfloat16)
        scaled_ref[...] = scaled.astype(jnp.float32)
        part = lax.dot_general(
            scaled, scaled, (((1,), (1,)), ((), ())), preferred_element_type=jnp.float32
        )
        gpart[...] = part.reshape(gpart.shape)

        def scatter(there):
            remote(gpart.at[there], rs.at[rank], 2, (at_core(0), there)).start()
            remote(
                gpart.at[chips + there, :, right], rs.at[rank, :, right], 2, (at_core(1), there)
            ).start()

        for there in chip_ids:
            scatter(there)

        @pl.when(core == 0)
        def _():
            remote(gpart.at[chips + p, :, right], rs.at[rank, :, right], 2, (at_core(1), p)).start()

        @pl.when(core == 1)
        def _():
            remote(gpart.at[p], rs.at[rank], 2, (at_core(0), p)).start()

        rs[rank] = gpart[rank]
        for there in team_ids[:-1]:
            give_energies(there)

        others = pl.ds(0, 2 * chips - 1)
        z_others = pl.ds(0, depth - 1)
        every = pl.ds(0, count)

        def across_z(part_of):
            landed(rs.at[others, :, part_of], 2)
            ar[z, :, part_of] = jnp.sum(rs[:, :, part_of], axis=0)
            for there in z_ids:
                remote(ar.at[z, :, part_of], ar.at[z, :, part_of], 3, (there, p)).start()

        def spread(part_of, mine_of, which):
            landed(ar.at[z_others, :, part_of], 3)
            mine_of[p] = jnp.sum(ar[:, :, part_of], axis=0)
            for there in chip_ids:
                for there_core in range(CORES):
                    remote(mine_of.at[p], mine_of.at[p], which, (at_core(there_core), there)).start()
            remote(mine_of.at[p], mine_of.at[p], which, (at_core(1 - core), p)).start()

        @pl.when(core == 0)
        def _():
            across_z(every)

        @pl.when(core == 1)
        def _():
            across_z(right)

        landed(ebuf.at[pl.ds(0, samp - 1)], 1)
        level = jnp.concatenate(
            [jnp.sum(ebuf[i * per : (i + 1) * per], axis=0) for i in range(samp // per)], axis=1
        )
        right_row = total_lanes(level) / count - level
        diagonal = lax.broadcasted_iota(jnp.int32, (count, count), 0) == lax.broadcasted_iota(
            jnp.int32, (count, count), 1
        )
        right_col = total_lanes(jnp.where(diagonal, right_row, 0.0))

        @pl.when(core == 0)
        def _():
            spread(every, top, 4)
            landed(top.at[pl.ds(0, chips - 1)], 4)
            landed(low, 5)

        @pl.when(core == 1)
        def _():
            spread(right, low, 5)
            landed(top, 4)
            landed(low.at[pl.ds(0, chips - 1)], 5)

        above = top[...].reshape(half, count)
        g_aa, g_ab = above[:, :half], above[:, half:]
        g_bb = low[...].reshape(half, half)
        g_ba = jnp.transpose(g_ab)
        cols = [right_col[:half], right_col[half:]]
        rows_of = [right_row[:, :half], right_row[:, half:]]
        d_row, r_row, d_col, r_col = rows_of, rows_of, cols, cols
        c_row = [jnp.zeros_like(v) for v in rows_of]
        c_col = [jnp.zeros_like(v) for v in cols]

        def inner(u, v):
            return total_lanes(u[0] * v[0] + u[1] * v[1])

        rr = inner(r_row, r_row)
        for turn in range(ITERS):
            image_row = [
                total_rows(g_aa * d_col[0] + g_ba * d_col[1]) + SHIFT * d_row[0],
                total_rows(g_ab * d_col[0] + g_bb * d_col[1]) + SHIFT * d_row[1],
            ]
            size = rr / inner(d_row, image_row)
            c_row = [c + size * d for c, d in zip(c_row, d_row)]
            c_col = [c + size * d for c, d in zip(c_col, d_col)]
            if turn == ITERS - 1:
                break
            image_col = [
                total_lanes(g_aa * d_row[0] + g_ab * d_row[1]) + SHIFT * d_col[0],
                total_lanes(g_ba * d_row[0] + g_bb * d_row[1]) + SHIFT * d_col[1],
            ]
            r_row = [r - size * v for r, v in zip(r_row, image_row)]
            r_col = [r - size * v for r, v in zip(r_col, image_col)]
            fresh = inner(r_row, r_row)
            ratio = fresh / rr
            d_row = [r + ratio * d for r, d in zip(r_row, d_row)]
            d_col = [r + ratio * d for r, d in zip(r_col, d_col)]
            rr = fresh

        c_row = jnp.concatenate(c_row, axis=1)

        update[s] = total_rows(scaled_ref[:half] * c_col[0] + scaled_ref[half:] * c_col[1])

        def give_piece(there):
            remote(update.at[s], update.at[s], 6, (there, p)).start()

        for there in team_ids[:-1]:
            give_piece(there)
            give_piece(there + team)
        give_piece(s + team)

        def own_samples(first):
            here = lax.rem(s, team) // per
            piece = c_row[:, first : first + LANES]
            for i in range(1, team // per):
                piece = jnp.where(here == i, c_row[:, first + i * LANES : first + (i + 1) * LANES], piece)
            return pltpu.roll(piece, lax.rem(LANES - offset, LANES), 1)

        cown[...] = own_samples(half)
        remote(cown, cbuf, 7, (s + team, p)).start()
        coeffs[...] = own_samples(0)[0, :rows]

        sent(jbuf.at[pl.ds(0, team - 1)], 0)
        sent(ebuf.at[pl.ds(0, team - 1)], 1)

        @pl.when(core == 0)
        def _():
            sent(gpart.at[pl.ds(0, chips - 1)], 2)
            sent(gpart.at[pl.ds(0, chips), :, right], 2)
            sent(ar.at[z_others], 3)
            sent(rs.at[others], 4)

        @pl.when(core == 1)
        def _():
            sent(gpart.at[pl.ds(0, chips)], 2)
            sent(gpart.at[pl.ds(0, chips - 1), :, right], 2)
            sent(ar.at[z_others, :, right], 3)
            sent(rs.at[others, :, right], 5)

        sent(update, 6)
        sent(update.at[pl.ds(0, team - 1)], 6)
        sent(cown, 7)
        landed(update.at[pl.ds(0, team - 1)], 6)


    @pl.when(sender)
    def _():
        pl.semaphore_wait(barrier, team)
        for there in team_ids:
            give_rows(there)
        sent(jbuf.at[pl.ds(0, team)], 0)
        for there in team_ids:
            give_energies(there)
        landed(cbuf, 7)
        coeffs[...] = cbuf[...][0, :rows]
        sent(ebuf.at[pl.ds(0, team)], 1)
        landed(update, 6)

    @pl.when(worker)
    def _():
        pl.semaphore_wait(barrier, team - 1 + par - 1)
        for there in team_ids[:-1]:
            give_rows(there)
        ebuf[s] = mine
        jbuf[s] = jown[s]
        landed(jbuf.at[pl.ds(0, samp - 1)], 0)
        work()


def hand_over_kernel(update, coeffs, update_out, coeffs_out, done):
    first = pltpu.make_async_copy(update, update_out, done.at[0])
    second = pltpu.make_async_copy(coeffs, coeffs_out, done.at[1])
    first.start()
    second.start()
    first.wait()
    second.wait()


def hand_over(update, coeffs):
    anywhere = pl.BlockSpec(memory_space=pl.ANY)
    return pl.pallas_call(
        hand_over_kernel,
        out_shape=(
            jax.ShapeDtypeStruct(update.shape, update.dtype),
            jax.ShapeDtypeStruct(coeffs.shape, coeffs.dtype),
        ),
        in_specs=[anywhere, anywhere],
        out_specs=(anywhere, anywhere),
        scratch_shapes=[pltpu.SemaphoreType.DMA((2,))],
        compiler_params=pltpu.CompilerParams(vmem_limit_bytes=VMEM_BYTES),
    )(update, coeffs)


def solution(mesh):
    samp, par = mesh.shape["samp"], mesh.shape["par"]
    chips = par
    depth = samp // (CORES * Y_HI)
    team = samp // Y_HI

    def per_device(jacobian, energies):
        rows, columns = jacobian.shape
        width = columns // team
        count = rows * samp
        half = count // 2
        share = half // chips
        update, coeffs = pl.pallas_call(
            functools.partial(kernel, samp, par),
            out_shape=(
                jax.ShapeDtypeStruct((team, 1, width), jnp.float32),
                jax.ShapeDtypeStruct((rows,), jnp.float32),
            ),
            in_specs=[
                pl.BlockSpec(memory_space=pl.ANY),
                pl.BlockSpec(memory_space=pl.ANY),
            ],
            out_specs=(
                pl.BlockSpec(memory_space=pltpu.VMEM),
                pl.BlockSpec(memory_space=pltpu.VMEM),
            ),
            scratch_shapes=[
                pltpu.VMEM((team, rows, width), jnp.float32),
                pltpu.SMEM((rows,), jnp.float32),
                pltpu.VMEM((samp, rows, width), jnp.float32),
                pltpu.VMEM((samp, 1, LANES), jnp.float32),
                pltpu.VMEM((1, LANES), jnp.float32),
                pltpu.VMEM((count, width), jnp.float32),
                pltpu.VMEM((2 * chips, share, count), jnp.float32),
                pltpu.VMEM((2 * chips, share, count), jnp.float32),
                pltpu.VMEM((depth, share, count), jnp.float32),
                pltpu.VMEM((chips, share, count), jnp.float32),
                pltpu.VMEM((chips, share, half), jnp.float32),
                pltpu.VMEM((1, LANES), jnp.float32),
                pltpu.VMEM((1, LANES), jnp.float32),
                pltpu.SemaphoreType.DMA((8,)),
                pltpu.SemaphoreType.DMA((8,)),
                pltpu.SemaphoreType.DMA((2,)),
            ],
            compiler_params=pltpu.CompilerParams(
                collective_id=0, has_side_effects=True, vmem_limit_bytes=VMEM_BYTES
            ),
        )(
            pltpu.with_memory_space_constraint(jacobian, pltpu.HBM),
            pltpu.with_memory_space_constraint(energies, pltpu.HBM),
        )
        return hand_over(update.reshape(columns), coeffs)

    return jax.shard_map(
        per_device,
        mesh=mesh,
        in_specs=(P("samp", "par"), P("samp")),
        out_specs=(P("par"), P("samp")),
        check_vma=False,
    )
```

```python
import functools

import jax
import jax.numpy as jnp
from jax import lax
from jax.experimental import pallas as pl
from jax.experimental.pallas import tpu as pltpu
from jax.sharding import PartitionSpec as P

P_SIZE = 65536
ITERS = 3
SHIFT = 0.05
CORES = 2
Y_HI = 2
Y_LO = 2
LANES = 128
VMEM_BYTES = 8 * 2**20
MESH = pl.DeviceIdType.MESH


def total_rows(block):
    return jnp.sum(block, axis=0, keepdims=True)


def total_lanes(block):
    return jnp.sum(block, axis=1, keepdims=True)


def each(count, body):
    def step(k, carry):
        body(k)
        return carry

    lax.fori_loop(0, count, step, 0)


def kernel(
    samp,
    par,
    jac,
    energies,
    update,
    coeffs,
    jown,
    elist,
    jbuf,
    ebuf,
    eown,
    scaled_ref,
    gpart,
    rs,
    ar,
    top,
    low,
    cown,
    cbuf,
    send,
    recv,
    local,
):
    depth = samp // (CORES * Y_HI)
    team = samp // Y_HI
    xs = par // Y_LO
    chips = par
    rows, width = jbuf.shape[1], jbuf.shape[2]
    count = samp * rows
    half = count // 2
    per = LANES // rows

    s = lax.axis_index("samp")
    p = lax.axis_index("par")
    core = lax.rem(s, CORES)
    z = lax.rem(s // CORES, depth)
    x = lax.rem(p, xs)
    y = p // xs
    rank = core * chips + p
    right = pl.ds(half, half)
    worker = s < team
    sender = jnp.logical_not(worker)

    def away(step, size):
        return min(step, size - step)

    x_at = [lax.rem(x + k, xs) for k in range(xs)]
    y_at = [y, 1 - y]
    z_at = [lax.rem(z + k, depth) for k in range(depth)]
    core_at = [core, 1 - core]
    z_steps = sorted(range(depth), key=lambda k: -away(k, depth))
    z_ids = [z_at[k] * CORES + core for k in z_steps[:-1]]
    team_ids = [z_at[k] * CORES + core_at[c] for k in z_steps for c in (1, 0)]
    by_core_ids = [z_at[k] * CORES + core_at[c] for c in (1, 0) for k in z_steps]
    fixed_core_ids = [z_at[k] * CORES + c for c in range(CORES) for k in z_steps]
    chip_steps = sorted(
        [(j, i) for j in range(Y_LO) for i in range(xs) if (j, i) != (0, 0)],
        key=lambda k: -k[0] - away(k[1], xs),
    )
    chip_ids = [y_at[j] * xs + x_at[i] for j, i in chip_steps]

    def at_core(there_core):
        return z * CORES + there_core

    def remote(src, dst, which, device):
        return pltpu.make_async_remote_copy(
            src_ref=src,
            dst_ref=dst,
            send_sem=send.at[which],
            recv_sem=recv.at[which],
            device_id=device,
            device_id_type=MESH,
        )

    def landed(block, which):
        pltpu.make_async_copy(block, block, recv.at[which]).wait()

    def sent(block, which):
        pltpu.make_async_copy(block, block, send.at[which]).wait()

    def columns(there):
        return jac.at[:, pl.ds(pl.multiple_of(there * width, width), width)]

    barrier = pltpu.get_barrier_semaphore()

    def greet(device):
        pl.semaphore_signal(barrier, inc=1, device_id=device, device_id_type=MESH)

    @pl.when(worker)
    def _():
        for there in team_ids:
            greet((there + team, p))
        for there in team_ids[:-1]:
            greet((there, p))
        each(par - 1, lambda k: greet((s, lax.rem(p + 1 + k, par))))

    def stage(there):
        pltpu.make_async_copy(columns(there), jown.at[there], local.at[0]).start()

    each(team, stage)
    level_copy = pltpu.make_async_copy(energies, elist, local.at[1])
    level_copy.start()
    level_copy.wait()
    lane = lax.broadcasted_iota(jnp.int32, (1, LANES), 1)
    offset = lax.rem(s * rows, LANES)
    mine = jnp.zeros((1, LANES), jnp.float32)
    for r in range(rows):
        mine = jnp.where(lane == offset + r, elist[r], mine)
    eown[...] = mine
    pltpu.make_async_copy(jown, jown, local.at[0]).wait()

    def give_rows(there):
        remote(jown.at[there], jbuf.at[s], 0, (there, p)).start()

    def give_energies(there):
        remote(eown, ebuf.at[s], 1, (there, p)).start()

    def work():
        block = jbuf[...].reshape(count, width)
        mean_col = total_rows(block) / count
        scaled = ((block - mean_col) * (1.0 / P_SIZE**0.5)).astype(jnp.bfloat16)
        scaled_ref[...] = scaled.astype(jnp.float32)
        part = lax.dot_general(
            scaled, scaled, (((1,), (1,)), ((), ())), preferred_element_type=jnp.float32
        )
        gpart[...] = part.reshape(gpart.shape)

        def scatter(there):
            remote(gpart.at[there], rs.at[rank], 2, (at_core(0), there)).start()
            remote(
                gpart.at[chips + there, :, right], rs.at[rank, :, right], 2, (at_core(1), there)
            ).start()

        for there in chip_ids:
            scatter(there)

        @pl.when(core == 0)
        def _():
            remote(gpart.at[chips + p, :, right], rs.at[rank, :, right], 2, (at_core(1), p)).start()

        @pl.when(core == 1)
        def _():
            remote(gpart.at[p], rs.at[rank], 2, (at_core(0), p)).start()

        rs[rank] = gpart[rank]
        for there in team_ids[:-1]:
            give_energies(there)

        others = pl.ds(0, 2 * chips - 1)
        z_others = pl.ds(0, depth - 1)
        every = pl.ds(0, count)

        def across_z(part_of):
            landed(rs.at[others, :, part_of], 2)
            ar[z, :, part_of] = jnp.sum(rs[:, :, part_of], axis=0)
            for there in z_ids:
                remote(ar.at[z, :, part_of], ar.at[z, :, part_of], 3, (there, p)).start()

        def spread(part_of, mine_of, which):
            landed(ar.at[z_others, :, part_of], 3)
            mine_of[p] = jnp.sum(ar[:, :, part_of], axis=0)
            for there_core in range(CORES):
                for there in chip_ids:
                    remote(mine_of.at[p], mine_of.at[p], which, (at_core(there_core), there)).start()
            remote(mine_of.at[p], mine_of.at[p], which, (at_core(1 - core), p)).start()

        @pl.when(core == 0)
        def _():
            across_z(every)

        @pl.when(core == 1)
        def _():
            across_z(right)

        landed(ebuf.at[pl.ds(0, samp - 1)], 1)
        level = jnp.concatenate(
            [jnp.sum(ebuf[i * per : (i + 1) * per], axis=0) for i in range(samp // per)], axis=1
        )
        right_row = total_lanes(level) / count - level
        diagonal = lax.broadcasted_iota(jnp.int32, (count, count), 0) == lax.broadcasted_iota(
            jnp.int32, (count, count), 1
        )
        right_col = total_lanes(jnp.where(diagonal, right_row, 0.0))

        @pl.when(core == 0)
        def _():
            spread(every, top, 4)
            landed(top.at[pl.ds(0, chips - 1)], 4)
            landed(low, 5)

        @pl.when(core == 1)
        def _():
            spread(right, low, 5)
            landed(top, 4)
            landed(low.at[pl.ds(0, chips - 1)], 5)

        above = top[...].reshape(half, count)
        g_aa, g_ab = above[:, :half], above[:, half:]
        g_bb = low[...].reshape(half, half)
        g_ba = jnp.transpose(g_ab)
        cols = [right_col[:half], right_col[half:]]
        rows_of = [right_row[:, :half], right_row[:, half:]]
        d_row, r_row, d_col, r_col = rows_of, rows_of, cols, cols
        c_row = [jnp.zeros_like(v) for v in rows_of]
        c_col = [jnp.zeros_like(v) for v in cols]

        def inner(u, v):
            return total_lanes(u[0] * v[0] + u[1] * v[1])

        rr = inner(r_row, r_row)
        for turn in range(ITERS):
            image_row = [
                total_rows(g_aa * d_col[0] + g_ba * d_col[1]) + SHIFT * d_row[0],
                total_rows(g_ab * d_col[0] + g_bb * d_col[1]) + SHIFT * d_row[1],
            ]
            size = rr / inner(d_row, image_row)
            c_row = [c + size * d for c, d in zip(c_row, d_row)]
            c_col = [c + size * d for c, d in zip(c_col, d_col)]
            if turn == ITERS - 1:
                break
            image_col = [
                total_lanes(g_aa * d_row[0] + g_ab * d_row[1]) + SHIFT * d_col[0],
                total_lanes(g_ba * d_row[0] + g_bb * d_row[1]) + SHIFT * d_col[1],
            ]
            r_row = [r - size * v for r, v in zip(r_row, image_row)]
            r_col = [r - size * v for r, v in zip(r_col, image_col)]
            fresh = inner(r_row, r_row)
            ratio = fresh / rr
            d_row = [r + ratio * d for r, d in zip(r_row, d_row)]
            d_col = [r + ratio * d for r, d in zip(r_col, d_col)]
            rr = fresh

        c_row = jnp.concatenate(c_row, axis=1)

        update[s] = total_rows(scaled_ref[:half] * c_col[0] + scaled_ref[half:] * c_col[1])

        def give_piece(there):
            remote(update.at[s], update.at[s], 6, (there, p)).start()

        for there in team_ids[:-1]:
            give_piece(there)
            give_piece(there + team)
        give_piece(s + team)

        def own_samples(first):
            here = lax.rem(s, team) // per
            piece = c_row[:, first : first + LANES]
            for i in range(1, team // per):
                piece = jnp.where(here == i, c_row[:, first + i * LANES : first + (i + 1) * LANES], piece)
            return pltpu.roll(piece, lax.rem(LANES - offset, LANES), 1)

        cown[...] = own_samples(half)
        remote(cown, cbuf, 7, (s + team, p)).start()
        coeffs[...] = own_samples(0)[0, :rows]

        sent(jbuf.at[pl.ds(0, team - 1)], 0)
        sent(ebuf.at[pl.ds(0, team - 1)], 1)

        @pl.when(core == 0)
        def _():
            sent(gpart.at[pl.ds(0, chips - 1)], 2)
            sent(gpart.at[pl.ds(0, chips), :, right], 2)
            sent(ar.at[z_others], 3)
            sent(rs.at[others], 4)

        @pl.when(core == 1)
        def _():
            sent(gpart.at[pl.ds(0, chips)], 2)
            sent(gpart.at[pl.ds(0, chips - 1), :, right], 2)
            sent(ar.at[z_others, :, right], 3)
            sent(rs.at[others, :, right], 5)

        sent(update, 6)
        sent(update.at[pl.ds(0, team - 1)], 6)
        sent(cown, 7)
        landed(update.at[pl.ds(0, team - 1)], 6)


    @pl.when(sender)
    def _():
        pl.semaphore_wait(barrier, team)
        for there in fixed_core_ids:
            give_rows(there)
        sent(jbuf.at[pl.ds(0, team)], 0)
        for there in team_ids:
            give_energies(there)
        landed(cbuf, 7)
        coeffs[...] = cbuf[...][0, :rows]
        sent(ebuf.at[pl.ds(0, team)], 1)
        landed(update, 6)

    @pl.when(worker)
    def _():
        pl.semaphore_wait(barrier, team - 1 + par - 1)
        for there in by_core_ids[:-1]:
            give_rows(there)
        ebuf[s] = mine
        jbuf[s] = jown[s]
        landed(jbuf.at[pl.ds(0, samp - 1)], 0)
        work()


def hand_over_kernel(update, coeffs, update_out, coeffs_out, done):
    first = pltpu.make_async_copy(update, update_out, done.at[0])
    second = pltpu.make_async_copy(coeffs, coeffs_out, done.at[1])
    first.start()
    second.start()
    first.wait()
    second.wait()


def hand_over(update, coeffs):
    anywhere = pl.BlockSpec(memory_space=pl.ANY)
    return pl.pallas_call(
        hand_over_kernel,
        out_shape=(
            jax.ShapeDtypeStruct(update.shape, update.dtype),
            jax.ShapeDtypeStruct(coeffs.shape, coeffs.dtype),
        ),
        in_specs=[anywhere, anywhere],
        out_specs=(anywhere, anywhere),
        scratch_shapes=[pltpu.SemaphoreType.DMA((2,))],
        compiler_params=pltpu.CompilerParams(vmem_limit_bytes=VMEM_BYTES),
    )(update, coeffs)


def solution(mesh):
    samp, par = mesh.shape["samp"], mesh.shape["par"]
    chips = par
    depth = samp // (CORES * Y_HI)
    team = samp // Y_HI

    def per_device(jacobian, energies):
        rows, columns = jacobian.shape
        width = columns // team
        count = rows * samp
        half = count // 2
        share = half // chips
        update, coeffs = pl.pallas_call(
            functools.partial(kernel, samp, par),
            out_shape=(
                jax.ShapeDtypeStruct((team, 1, width), jnp.float32),
                jax.ShapeDtypeStruct((rows,), jnp.float32),
            ),
            in_specs=[
                pl.BlockSpec(memory_space=pl.ANY),
                pl.BlockSpec(memory_space=pl.ANY),
            ],
            out_specs=(
                pl.BlockSpec(memory_space=pltpu.VMEM),
                pl.BlockSpec(memory_space=pltpu.VMEM),
            ),
            scratch_shapes=[
                pltpu.VMEM((team, rows, width), jnp.float32),
                pltpu.SMEM((rows,), jnp.float32),
                pltpu.VMEM((samp, rows, width), jnp.float32),
                pltpu.VMEM((samp, 1, LANES), jnp.float32),
                pltpu.VMEM((1, LANES), jnp.float32),
                pltpu.VMEM((count, width), jnp.float32),
                pltpu.VMEM((2 * chips, share, count), jnp.float32),
                pltpu.VMEM((2 * chips, share, count), jnp.float32),
                pltpu.VMEM((depth, share, count), jnp.float32),
                pltpu.VMEM((chips, share, count), jnp.float32),
                pltpu.VMEM((chips, share, half), jnp.float32),
                pltpu.VMEM((1, LANES), jnp.float32),
                pltpu.VMEM((1, LANES), jnp.float32),
                pltpu.SemaphoreType.DMA((8,)),
                pltpu.SemaphoreType.DMA((8,)),
                pltpu.SemaphoreType.DMA((2,)),
            ],
            compiler_params=pltpu.CompilerParams(
                collective_id=0, has_side_effects=True, vmem_limit_bytes=VMEM_BYTES
            ),
        )(
            pltpu.with_memory_space_constraint(jacobian, pltpu.HBM),
            pltpu.with_memory_space_constraint(energies, pltpu.HBM),
        )
        return hand_over(update.reshape(columns), coeffs)

    return jax.shard_map(
        per_device,
        mesh=mesh,
        in_specs=(P("samp", "par"), P("samp")),
        out_specs=(P("par"), P("samp")),
        check_vma=False,
    )
```

```python
import functools

import jax
import jax.numpy as jnp
from jax import lax
from jax.experimental import pallas as pl
from jax.experimental.pallas import tpu as pltpu
from jax.sharding import PartitionSpec as P

P_SIZE = 65536
ITERS = 3
SHIFT = 0.05
CORES = 2
Y_HI = 2
Y_LO = 2
LANES = 128
VMEM_BYTES = 8 * 2**20
MESH = pl.DeviceIdType.MESH


def total_rows(block):
    return jnp.sum(block, axis=0, keepdims=True)


def total_lanes(block):
    return jnp.sum(block, axis=1, keepdims=True)


def each(count, body):
    def step(k, carry):
        body(k)
        return carry

    lax.fori_loop(0, count, step, 0)


def kernel(
    samp,
    par,
    jac,
    energies,
    update,
    coeffs,
    jown,
    elist,
    jbuf,
    ebuf,
    eown,
    scaled_ref,
    gpart,
    rs,
    ar,
    top,
    low,
    cown,
    cbuf,
    send,
    recv,
    local,
):
    depth = samp // (CORES * Y_HI)
    team = samp // Y_HI
    xs = par // Y_LO
    chips = par
    rows, width = jbuf.shape[1], jbuf.shape[2]
    count = samp * rows
    half = count // 2
    per = LANES // rows

    s = lax.axis_index("samp")
    p = lax.axis_index("par")
    core = lax.rem(s, CORES)
    z = lax.rem(s // CORES, depth)
    x = lax.rem(p, xs)
    y = p // xs
    rank = core * chips + p
    right = pl.ds(half, half)
    worker = s < team
    sender = jnp.logical_not(worker)

    def away(step, size):
        return min(step, size - step)

    x_at = [lax.rem(x + k, xs) for k in range(xs)]
    y_at = [y, 1 - y]
    z_at = [lax.rem(z + k, depth) for k in range(depth)]
    core_at = [core, 1 - core]
    z_steps = sorted(range(depth), key=lambda k: -away(k, depth))
    z_ids = [z_at[k] * CORES + core for k in z_steps[:-1]]
    team_ids = [z_at[k] * CORES + core_at[c] for k in z_steps for c in (1, 0)]
    by_core_ids = [z_at[k] * CORES + core_at[c] for c in (1, 0) for k in z_steps]
    fixed_core_ids = [z_at[k] * CORES + c for c in range(CORES) for k in z_steps]
    chip_steps = sorted(
        [(j, i) for j in range(Y_LO) for i in range(xs) if (j, i) != (0, 0)],
        key=lambda k: -k[0] - away(k[1], xs),
    )
    chip_ids = [y_at[j] * xs + x_at[i] for j, i in chip_steps]

    def at_core(there_core):
        return z * CORES + there_core

    def remote(src, dst, which, device):
        return pltpu.make_async_remote_copy(
            src_ref=src,
            dst_ref=dst,
            send_sem=send.at[which],
            recv_sem=recv.at[which],
            device_id=device,
            device_id_type=MESH,
        )

    def landed(block, which):
        pltpu.make_async_copy(block, block, recv.at[which]).wait()

    def sent(block, which):
        pltpu.make_async_copy(block, block, send.at[which]).wait()

    def columns(there):
        return jac.at[:, pl.ds(pl.multiple_of(there * width, width), width)]

    barrier = pltpu.get_barrier_semaphore()

    def greet(device):
        pl.semaphore_signal(barrier, inc=1, device_id=device, device_id_type=MESH)

    @pl.when(worker)
    def _():
        for there in team_ids:
            greet((there + team, p))
        for there in team_ids[:-1]:
            greet((there, p))
        each(par - 1, lambda k: greet((s, lax.rem(p + 1 + k, par))))

    def stage(there):
        pltpu.make_async_copy(columns(there), jown.at[there], local.at[0]).start()

    each(team, stage)
    level_copy = pltpu.make_async_copy(energies, elist, local.at[1])
    level_copy.start()
    level_copy.wait()
    lane = lax.broadcasted_iota(jnp.int32, (1, LANES), 1)
    offset = lax.rem(s * rows, LANES)
    mine = jnp.zeros((1, LANES), jnp.float32)
    for r in range(rows):
        mine = jnp.where(lane == offset + r, elist[r], mine)
    eown[...] = mine
    pltpu.make_async_copy(jown, jown, local.at[0]).wait()

    def give_rows(there):
        remote(jown.at[there], jbuf.at[s], 0, (there, p)).start()

    def give_energies(there):
        remote(eown, ebuf.at[s], 1, (there, p)).start()

    def work():
        block = jbuf[...].reshape(count, width)
        mean_col = total_rows(block) / count
        scaled = ((block - mean_col) * (1.0 / P_SIZE**0.5)).astype(jnp.bfloat16)
        scaled_ref[...] = scaled.astype(jnp.float32)
        part = lax.dot_general(
            scaled, scaled, (((1,), (1,)), ((), ())), preferred_element_type=jnp.float32
        )
        gpart[...] = part.reshape(gpart.shape)

        def scatter(there):
            remote(gpart.at[there], rs.at[rank], 2, (at_core(0), there)).start()
            remote(
                gpart.at[chips + there, :, right], rs.at[rank, :, right], 2, (at_core(1), there)
            ).start()

        for there in chip_ids:
            scatter(there)

        @pl.when(core == 0)
        def _():
            remote(gpart.at[chips + p, :, right], rs.at[rank, :, right], 2, (at_core(1), p)).start()

        @pl.when(core == 1)
        def _():
            remote(gpart.at[p], rs.at[rank], 2, (at_core(0), p)).start()

        rs[rank] = gpart[rank]
        for there in team_ids[:-1]:
            give_energies(there)

        others = pl.ds(0, 2 * chips - 1)
        z_others = pl.ds(0, depth - 1)
        every = pl.ds(0, count)

        def across_z(part_of):
            landed(rs.at[others, :, part_of], 2)
            ar[z, :, part_of] = jnp.sum(rs[:, :, part_of], axis=0)
            for there in z_ids:
                remote(ar.at[z, :, part_of], ar.at[z, :, part_of], 3, (there, p)).start()

        def spread(part_of, mine_of, which):
            landed(ar.at[z_others, :, part_of], 3)
            mine_of[p] = jnp.sum(ar[:, :, part_of], axis=0)
            for there_core in range(CORES):
                for there in chip_ids:
                    remote(mine_of.at[p], mine_of.at[p], which, (at_core(there_core), there)).start()
            remote(mine_of.at[p], mine_of.at[p], which, (at_core(1 - core), p)).start()

        @pl.when(core == 0)
        def _():
            across_z(every)

        @pl.when(core == 1)
        def _():
            across_z(right)

        landed(ebuf.at[pl.ds(0, samp - 1)], 1)
        level = jnp.concatenate(
            [jnp.sum(ebuf[i * per : (i + 1) * per], axis=0) for i in range(samp // per)], axis=1
        )
        right_row = total_lanes(level) / count - level
        diagonal = lax.broadcasted_iota(jnp.int32, (count, count), 0) == lax.broadcasted_iota(
            jnp.int32, (count, count), 1
        )
        right_col = total_lanes(jnp.where(diagonal, right_row, 0.0))

        @pl.when(core == 0)
        def _():
            spread(every, top, 4)
            landed(top.at[pl.ds(0, chips - 1)], 4)
            landed(low, 5)

        @pl.when(core == 1)
        def _():
            spread(right, low, 5)
            landed(top, 4)
            landed(low.at[pl.ds(0, chips - 1)], 5)

        above = top[...].reshape(half, count)
        g_aa, g_ab = above[:, :half], above[:, half:]
        g_bb = low[...].reshape(half, half)
        g_ba = jnp.transpose(g_ab)
        cols = [right_col[:half], right_col[half:]]
        rows_of = [right_row[:, :half], right_row[:, half:]]
        d_row, r_row, d_col, r_col = rows_of, rows_of, cols, cols
        c_row = [jnp.zeros_like(v) for v in rows_of]
        c_col = [jnp.zeros_like(v) for v in cols]

        def inner(u, v):
            return total_lanes(u[0] * v[0] + u[1] * v[1])

        rr = inner(r_row, r_row)
        for turn in range(ITERS):
            image_row = [
                total_rows(g_aa * d_col[0] + g_ba * d_col[1]) + SHIFT * d_row[0],
                total_rows(g_ab * d_col[0] + g_bb * d_col[1]) + SHIFT * d_row[1],
            ]
            size = rr / inner(d_row, image_row)
            c_row = [c + size * d for c, d in zip(c_row, d_row)]
            c_col = [c + size * d for c, d in zip(c_col, d_col)]
            if turn == ITERS - 1:
                break
            image_col = [
                total_lanes(g_aa * d_row[0] + g_ab * d_row[1]) + SHIFT * d_col[0],
                total_lanes(g_ba * d_row[0] + g_bb * d_row[1]) + SHIFT * d_col[1],
            ]
            r_row = [r - size * v for r, v in zip(r_row, image_row)]
            r_col = [r - size * v for r, v in zip(r_col, image_col)]
            fresh = inner(r_row, r_row)
            ratio = fresh / rr
            d_row = [r + ratio * d for r, d in zip(r_row, d_row)]
            d_col = [r + ratio * d for r, d in zip(r_col, d_col)]
            rr = fresh

        c_row = jnp.concatenate(c_row, axis=1)

        update[s] = total_rows(scaled_ref[:half] * c_col[0] + scaled_ref[half:] * c_col[1])

        def give_piece(there):
            remote(update.at[s], update.at[s], 6, (there, p)).start()

        for there in team_ids[:-1]:
            give_piece(there)
            give_piece(there + team)
        give_piece(s + team)

        def own_samples(first):
            here = lax.rem(s, team) // per
            piece = c_row[:, first : first + LANES]
            for i in range(1, team // per):
                piece = jnp.where(here == i, c_row[:, first + i * LANES : first + (i + 1) * LANES], piece)
            return pltpu.roll(piece, lax.rem(LANES - offset, LANES), 1)

        cown[...] = own_samples(half)
        remote(cown, cbuf, 7, (s + team, p)).start()
        coeffs[...] = own_samples(0)[0, :rows]

        sent(jbuf.at[pl.ds(0, team - 1)], 0)
        sent(ebuf.at[pl.ds(0, team - 1)], 1)

        @pl.when(core == 0)
        def _():
            sent(gpart.at[pl.ds(0, chips - 1)], 2)
            sent(gpart.at[pl.ds(0, chips), :, right], 2)
            sent(ar.at[z_others], 3)
            sent(rs.at[others], 4)

        @pl.when(core == 1)
        def _():
            sent(gpart.at[pl.ds(0, chips)], 2)
            sent(gpart.at[pl.ds(0, chips - 1), :, right], 2)
            sent(ar.at[z_others, :, right], 3)
            sent(rs.at[others, :, right], 5)

        sent(update, 6)
        sent(update.at[pl.ds(0, team - 1)], 6)
        sent(cown, 7)
        landed(update.at[pl.ds(0, team - 1)], 6)


    @pl.when(sender)
    def _():
        pl.semaphore_wait(barrier, team)
        for there in fixed_core_ids:
            give_rows(there)
        sent(jbuf.at[pl.ds(0, team)], 0)
        for there in team_ids:
            give_energies(there)
        landed(cbuf, 7)
        coeffs[...] = cbuf[...][0, :rows]
        sent(ebuf.at[pl.ds(0, team)], 1)
        landed(update, 6)

    @pl.when(worker)
    def _():
        pl.semaphore_wait(barrier, team - 1 + par - 1)
        for there in fixed_core_ids:

            @pl.when(there != s)
            def _(there=there):
                give_rows(there)

        ebuf[s] = mine
        jbuf[s] = jown[s]
        landed(jbuf.at[pl.ds(0, samp - 1)], 0)
        work()


def hand_over_kernel(update, coeffs, update_out, coeffs_out, done):
    first = pltpu.make_async_copy(update, update_out, done.at[0])
    second = pltpu.make_async_copy(coeffs, coeffs_out, done.at[1])
    first.start()
    second.start()
    first.wait()
    second.wait()


def hand_over(update, coeffs):
    anywhere = pl.BlockSpec(memory_space=pl.ANY)
    return pl.pallas_call(
        hand_over_kernel,
        out_shape=(
            jax.ShapeDtypeStruct(update.shape, update.dtype),
            jax.ShapeDtypeStruct(coeffs.shape, coeffs.dtype),
        ),
        in_specs=[anywhere, anywhere],
        out_specs=(anywhere, anywhere),
        scratch_shapes=[pltpu.SemaphoreType.DMA((2,))],
        compiler_params=pltpu.CompilerParams(vmem_limit_bytes=VMEM_BYTES),
    )(update, coeffs)


def solution(mesh):
    samp, par = mesh.shape["samp"], mesh.shape["par"]
    chips = par
    depth = samp // (CORES * Y_HI)
    team = samp // Y_HI

    def per_device(jacobian, energies):
        rows, columns = jacobian.shape
        width = columns // team
        count = rows * samp
        half = count // 2
        share = half // chips
        update, coeffs = pl.pallas_call(
            functools.partial(kernel, samp, par),
            out_shape=(
                jax.ShapeDtypeStruct((team, 1, width), jnp.float32),
                jax.ShapeDtypeStruct((rows,), jnp.float32),
            ),
            in_specs=[
                pl.BlockSpec(memory_space=pl.ANY),
                pl.BlockSpec(memory_space=pl.ANY),
            ],
            out_specs=(
                pl.BlockSpec(memory_space=pltpu.VMEM),
                pl.BlockSpec(memory_space=pltpu.VMEM),
            ),
            scratch_shapes=[
                pltpu.VMEM((team, rows, width), jnp.float32),
                pltpu.SMEM((rows,), jnp.float32),
                pltpu.VMEM((samp, rows, width), jnp.float32),
                pltpu.VMEM((samp, 1, LANES), jnp.float32),
                pltpu.VMEM((1, LANES), jnp.float32),
                pltpu.VMEM((count, width), jnp.float32),
                pltpu.VMEM((2 * chips, share, count), jnp.float32),
                pltpu.VMEM((2 * chips, share, count), jnp.float32),
                pltpu.VMEM((depth, share, count), jnp.float32),
                pltpu.VMEM((chips, share, count), jnp.float32),
                pltpu.VMEM((chips, share, half), jnp.float32),
                pltpu.VMEM((1, LANES), jnp.float32),
                pltpu.VMEM((1, LANES), jnp.float32),
                pltpu.SemaphoreType.DMA((8,)),
                pltpu.SemaphoreType.DMA((8,)),
                pltpu.SemaphoreType.DMA((2,)),
            ],
            compiler_params=pltpu.CompilerParams(
                collective_id=0, has_side_effects=True, vmem_limit_bytes=VMEM_BYTES
            ),
        )(
            pltpu.with_memory_space_constraint(jacobian, pltpu.HBM),
            pltpu.with_memory_space_constraint(energies, pltpu.HBM),
        )
        return hand_over(update.reshape(columns), coeffs)

    return jax.shard_map(
        per_device,
        mesh=mesh,
        in_specs=(P("samp", "par"), P("samp")),
        out_specs=(P("par"), P("samp")),
        check_vma=False,
    )
```

```python
import functools

import jax
import jax.numpy as jnp
from jax import lax
from jax.experimental import pallas as pl
from jax.experimental.pallas import tpu as pltpu
from jax.sharding import PartitionSpec as P

P_SIZE = 65536
ITERS = 3
SHIFT = 0.05
CORES = 2
Y_HI = 2
Y_LO = 2
LANES = 128
VMEM_BYTES = 8 * 2**20
MESH = pl.DeviceIdType.MESH


def total_rows(block):
    return jnp.sum(block, axis=0, keepdims=True)


def total_lanes(block):
    return jnp.sum(block, axis=1, keepdims=True)


def each(count, body):
    def step(k, carry):
        body(k)
        return carry

    lax.fori_loop(0, count, step, 0)


def kernel(
    samp,
    par,
    jac,
    energies,
    update,
    coeffs,
    jown,
    elist,
    jbuf,
    ebuf,
    eown,
    scaled_ref,
    gpart,
    rs,
    ar,
    top,
    low,
    cown,
    cbuf,
    send,
    recv,
    local,
):
    depth = samp // (CORES * Y_HI)
    team = samp // Y_HI
    xs = par // Y_LO
    chips = par
    rows, width = jbuf.shape[1], jbuf.shape[2]
    count = samp * rows
    half = count // 2
    per = LANES // rows

    s = lax.axis_index("samp")
    p = lax.axis_index("par")
    core = lax.rem(s, CORES)
    z = lax.rem(s // CORES, depth)
    x = lax.rem(p, xs)
    y = p // xs
    rank = core * chips + p
    right = pl.ds(half, half)
    worker = s < team
    sender = jnp.logical_not(worker)

    def away(step, size):
        return min(step, size - step)

    x_at = [lax.rem(x + k, xs) for k in range(xs)]
    y_at = [y, 1 - y]
    z_at = [lax.rem(z + k, depth) for k in range(depth)]
    core_at = [core, 1 - core]
    z_steps = sorted(range(depth), key=lambda k: -away(k, depth))
    z_ids = [z_at[k] * CORES + core for k in z_steps[:-1]]
    team_ids = [z_at[k] * CORES + core_at[c] for k in z_steps for c in (1, 0)]
    by_core_ids = [z_at[k] * CORES + core_at[c] for c in (1, 0) for k in z_steps]
    fixed_core_ids = [z_at[k] * CORES + c for c in range(CORES) for k in z_steps]
    chip_steps = sorted(
        [(j, i) for j in range(Y_LO) for i in range(xs) if (j, i) != (0, 0)],
        key=lambda k: -k[0] - away(k[1], xs),
    )
    chip_ids = [y_at[j] * xs + x_at[i] for j, i in chip_steps]

    def at_core(there_core):
        return z * CORES + there_core

    def remote(src, dst, which, device):
        return pltpu.make_async_remote_copy(
            src_ref=src,
            dst_ref=dst,
            send_sem=send.at[which],
            recv_sem=recv.at[which],
            device_id=device,
            device_id_type=MESH,
        )

    def landed(block, which):
        pltpu.make_async_copy(block, block, recv.at[which]).wait()

    def sent(block, which):
        pltpu.make_async_copy(block, block, send.at[which]).wait()

    def columns(there):
        return jac.at[:, pl.ds(pl.multiple_of(there * width, width), width)]

    barrier = pltpu.get_barrier_semaphore()

    def greet(device):
        pl.semaphore_signal(barrier, inc=1, device_id=device, device_id_type=MESH)

    @pl.when(worker)
    def _():
        for there in team_ids:
            greet((there + team, p))
        for there in team_ids[:-1]:
            greet((there, p))
        each(par - 1, lambda k: greet((s, lax.rem(p + 1 + k, par))))

    def stage(there):
        pltpu.make_async_copy(columns(there), jown.at[there], local.at[0]).start()

    each(team, stage)
    level_copy = pltpu.make_async_copy(energies, elist, local.at[1])
    level_copy.start()
    level_copy.wait()
    lane = lax.broadcasted_iota(jnp.int32, (1, LANES), 1)
    offset = lax.rem(s * rows, LANES)
    mine = jnp.zeros((1, LANES), jnp.float32)
    for r in range(rows):
        mine = jnp.where(lane == offset + r, elist[r], mine)
    eown[...] = mine
    pltpu.make_async_copy(jown, jown, local.at[0]).wait()

    def give_rows(there):
        remote(jown.at[there], jbuf.at[s], 0, (there, p)).start()

    def give_energies(there):
        remote(eown, ebuf.at[s], 1, (there, p)).start()

    def work():
        block = jbuf[...].reshape(count, width)
        mean_col = total_rows(block) / count
        scaled = ((block - mean_col) * (1.0 / P_SIZE**0.5)).astype(jnp.bfloat16)
        scaled_ref[...] = scaled.astype(jnp.float32)
        part = lax.dot_general(
            scaled, scaled, (((1,), (1,)), ((), ())), preferred_element_type=jnp.float32
        )
        gpart[...] = part.reshape(gpart.shape)

        def scatter(there):
            remote(gpart.at[there], rs.at[rank], 2, (at_core(0), there)).start()
            remote(
                gpart.at[chips + there, :, right], rs.at[rank, :, right], 2, (at_core(1), there)
            ).start()

        for there in chip_ids:
            scatter(there)

        @pl.when(core == 0)
        def _():
            remote(gpart.at[chips + p, :, right], rs.at[rank, :, right], 2, (at_core(1), p)).start()

        @pl.when(core == 1)
        def _():
            remote(gpart.at[p], rs.at[rank], 2, (at_core(0), p)).start()

        rs[rank] = gpart[rank]
        for there in team_ids[:-1]:
            give_energies(there)

        others = pl.ds(0, 2 * chips - 1)
        z_others = pl.ds(0, depth - 1)
        every = pl.ds(0, count)

        def across_z(part_of):
            landed(rs.at[others, :, part_of], 2)
            ar[z, :, part_of] = jnp.sum(rs[:, :, part_of], axis=0)
            for there in z_ids:
                remote(ar.at[z, :, part_of], ar.at[z, :, part_of], 3, (there, p)).start()

        def spread(part_of, mine_of, which):
            landed(ar.at[z_others, :, part_of], 3)
            mine_of[p] = jnp.sum(ar[:, :, part_of], axis=0)
            for there_core in range(CORES):
                for there in chip_ids:
                    remote(mine_of.at[p], mine_of.at[p], which, (at_core(there_core), there)).start()
            remote(mine_of.at[p], mine_of.at[p], which, (at_core(1 - core), p)).start()

        @pl.when(core == 0)
        def _():
            across_z(every)

        @pl.when(core == 1)
        def _():
            across_z(right)

        landed(ebuf.at[pl.ds(0, samp - 1)], 1)
        level = jnp.concatenate(
            [jnp.sum(ebuf[i * per : (i + 1) * per], axis=0) for i in range(samp // per)], axis=1
        )
        right_row = total_lanes(level) / count - level
        diagonal = lax.broadcasted_iota(jnp.int32, (count, count), 0) == lax.broadcasted_iota(
            jnp.int32, (count, count), 1
        )
        right_col = total_lanes(jnp.where(diagonal, right_row, 0.0))

        @pl.when(core == 0)
        def _():
            spread(every, top, 4)
            landed(top.at[pl.ds(0, chips - 1)], 4)
            landed(low, 5)

        @pl.when(core == 1)
        def _():
            spread(right, low, 5)
            landed(top, 4)
            landed(low.at[pl.ds(0, chips - 1)], 5)

        above = top[...].reshape(half, count)
        g_aa, g_ab = above[:, :half], above[:, half:]
        g_bb = low[...].reshape(half, half)
        g_ba = jnp.transpose(g_ab)
        cols = [right_col[:half], right_col[half:]]
        rows_of = [right_row[:, :half], right_row[:, half:]]
        d_row, r_row, d_col, r_col = rows_of, rows_of, cols, cols
        c_row = [jnp.zeros_like(v) for v in rows_of]
        c_col = [jnp.zeros_like(v) for v in cols]

        def inner(u, v):
            return total_lanes(u[0] * v[0] + u[1] * v[1])

        rr = inner(r_row, r_row)
        for turn in range(ITERS):
            image_row = [
                total_rows(g_aa * d_col[0] + g_ba * d_col[1]) + SHIFT * d_row[0],
                total_rows(g_ab * d_col[0] + g_bb * d_col[1]) + SHIFT * d_row[1],
            ]
            size = rr / inner(d_row, image_row)
            c_row = [c + size * d for c, d in zip(c_row, d_row)]
            c_col = [c + size * d for c, d in zip(c_col, d_col)]
            if turn == ITERS - 1:
                break
            image_col = [
                total_lanes(g_aa * d_row[0] + g_ab * d_row[1]) + SHIFT * d_col[0],
                total_lanes(g_ba * d_row[0] + g_bb * d_row[1]) + SHIFT * d_col[1],
            ]
            r_row = [r - size * v for r, v in zip(r_row, image_row)]
            r_col = [r - size * v for r, v in zip(r_col, image_col)]
            fresh = inner(r_row, r_row)
            ratio = fresh / rr
            d_row = [r + ratio * d for r, d in zip(r_row, d_row)]
            d_col = [r + ratio * d for r, d in zip(r_col, d_col)]
            rr = fresh

        c_row = jnp.concatenate(c_row, axis=1)

        update[s] = total_rows(scaled_ref[:half] * c_col[0] + scaled_ref[half:] * c_col[1])

        def give_piece(there):
            remote(update.at[s], update.at[s], 6, (there, p)).start()

        for there in [z_at[k] * CORES + c for c in reversed(range(CORES)) for k in z_steps]:

            @pl.when(there != s)
            def _(there=there):
                give_piece(there)

            give_piece(there + team)


        def own_samples(first):
            here = lax.rem(s, team) // per
            piece = c_row[:, first : first + LANES]
            for i in range(1, team // per):
                piece = jnp.where(here == i, c_row[:, first + i * LANES : first + (i + 1) * LANES], piece)
            return pltpu.roll(piece, lax.rem(LANES - offset, LANES), 1)

        cown[...] = own_samples(half)
        remote(cown, cbuf, 7, (s + team, p)).start()
        coeffs[...] = own_samples(0)[0, :rows]

        sent(jbuf.at[pl.ds(0, team - 1)], 0)
        sent(ebuf.at[pl.ds(0, team - 1)], 1)

        @pl.when(core == 0)
        def _():
            sent(gpart.at[pl.ds(0, chips - 1)], 2)
            sent(gpart.at[pl.ds(0, chips), :, right], 2)
            sent(ar.at[z_others], 3)
            sent(rs.at[others], 4)

        @pl.when(core == 1)
        def _():
            sent(gpart.at[pl.ds(0, chips)], 2)
            sent(gpart.at[pl.ds(0, chips - 1), :, right], 2)
            sent(ar.at[z_others, :, right], 3)
            sent(rs.at[others, :, right], 5)

        sent(update, 6)
        sent(update.at[pl.ds(0, team - 1)], 6)
        sent(cown, 7)
        landed(update.at[pl.ds(0, team - 1)], 6)


    @pl.when(sender)
    def _():
        pl.semaphore_wait(barrier, team)
        for there in fixed_core_ids:
            give_rows(there)
        sent(jbuf.at[pl.ds(0, team)], 0)
        for there in team_ids:
            give_energies(there)
        landed(cbuf, 7)
        coeffs[...] = cbuf[...][0, :rows]
        sent(ebuf.at[pl.ds(0, team)], 1)
        landed(update, 6)

    @pl.when(worker)
    def _():
        pl.semaphore_wait(barrier, team - 1 + par - 1)
        for there in by_core_ids[:-1]:
            give_rows(there)
        ebuf[s] = mine
        jbuf[s] = jown[s]
        landed(jbuf.at[pl.ds(0, samp - 1)], 0)
        work()


def hand_over_kernel(update, coeffs, update_out, coeffs_out, done):
    first = pltpu.make_async_copy(update, update_out, done.at[0])
    second = pltpu.make_async_copy(coeffs, coeffs_out, done.at[1])
    first.start()
    second.start()
    first.wait()
    second.wait()


def hand_over(update, coeffs):
    anywhere = pl.BlockSpec(memory_space=pl.ANY)
    return pl.pallas_call(
        hand_over_kernel,
        out_shape=(
            jax.ShapeDtypeStruct(update.shape, update.dtype),
            jax.ShapeDtypeStruct(coeffs.shape, coeffs.dtype),
        ),
        in_specs=[anywhere, anywhere],
        out_specs=(anywhere, anywhere),
        scratch_shapes=[pltpu.SemaphoreType.DMA((2,))],
        compiler_params=pltpu.CompilerParams(vmem_limit_bytes=VMEM_BYTES),
    )(update, coeffs)


def solution(mesh):
    samp, par = mesh.shape["samp"], mesh.shape["par"]
    chips = par
    depth = samp // (CORES * Y_HI)
    team = samp // Y_HI

    def per_device(jacobian, energies):
        rows, columns = jacobian.shape
        width = columns // team
        count = rows * samp
        half = count // 2
        share = half // chips
        update, coeffs = pl.pallas_call(
            functools.partial(kernel, samp, par),
            out_shape=(
                jax.ShapeDtypeStruct((team, 1, width), jnp.float32),
                jax.ShapeDtypeStruct((rows,), jnp.float32),
            ),
            in_specs=[
                pl.BlockSpec(memory_space=pl.ANY),
                pl.BlockSpec(memory_space=pl.ANY),
            ],
            out_specs=(
                pl.BlockSpec(memory_space=pltpu.VMEM),
                pl.BlockSpec(memory_space=pltpu.VMEM),
            ),
            scratch_shapes=[
                pltpu.VMEM((team, rows, width), jnp.float32),
                pltpu.SMEM((rows,), jnp.float32),
                pltpu.VMEM((samp, rows, width), jnp.float32),
                pltpu.VMEM((samp, 1, LANES), jnp.float32),
                pltpu.VMEM((1, LANES), jnp.float32),
                pltpu.VMEM((count, width), jnp.float32),
                pltpu.VMEM((2 * chips, share, count), jnp.float32),
                pltpu.VMEM((2 * chips, share, count), jnp.float32),
                pltpu.VMEM((depth, share, count), jnp.float32),
                pltpu.VMEM((chips, share, count), jnp.float32),
                pltpu.VMEM((chips, share, half), jnp.float32),
                pltpu.VMEM((1, LANES), jnp.float32),
                pltpu.VMEM((1, LANES), jnp.float32),
                pltpu.SemaphoreType.DMA((8,)),
                pltpu.SemaphoreType.DMA((8,)),
                pltpu.SemaphoreType.DMA((2,)),
            ],
            compiler_params=pltpu.CompilerParams(
                collective_id=0, has_side_effects=True, vmem_limit_bytes=VMEM_BYTES
            ),
        )(
            pltpu.with_memory_space_constraint(jacobian, pltpu.HBM),
            pltpu.with_memory_space_constraint(energies, pltpu.HBM),
        )
        return hand_over(update.reshape(columns), coeffs)

    return jax.shard_map(
        per_device,
        mesh=mesh,
        in_specs=(P("samp", "par"), P("samp")),
        out_specs=(P("par"), P("samp")),
        check_vma=False,
    )
```

```python
import functools

import jax
import jax.numpy as jnp
from jax import lax
from jax.experimental import pallas as pl
from jax.experimental.pallas import tpu as pltpu
from jax.sharding import PartitionSpec as P

P_SIZE = 65536
ITERS = 3
SHIFT = 0.05
CORES = 2
Y_HI = 2
Y_LO = 2
LANES = 128
VMEM_BYTES = 8 * 2**20
MESH = pl.DeviceIdType.MESH


def total_rows(block):
    return jnp.sum(block, axis=0, keepdims=True)


def total_lanes(block):
    return jnp.sum(block, axis=1, keepdims=True)


def each(count, body):
    def step(k, carry):
        body(k)
        return carry

    lax.fori_loop(0, count, step, 0)


def kernel(
    samp,
    par,
    jac,
    energies,
    update,
    coeffs,
    jown,
    elist,
    jbuf,
    ebuf,
    eown,
    scaled_ref,
    gpart,
    rs,
    ar,
    top,
    low,
    cown,
    cbuf,
    send,
    recv,
    local,
):
    depth = samp // (CORES * Y_HI)
    team = samp // Y_HI
    xs = par // Y_LO
    chips = par
    rows, width = jbuf.shape[1], jbuf.shape[2]
    count = samp * rows
    half = count // 2
    per = LANES // rows

    s = lax.axis_index("samp")
    p = lax.axis_index("par")
    core = lax.rem(s, CORES)
    z = lax.rem(s // CORES, depth)
    x = lax.rem(p, xs)
    y = p // xs
    rank = core * chips + p
    right = pl.ds(half, half)
    worker = s < team
    sender = jnp.logical_not(worker)

    def away(step, size):
        return min(step, size - step)

    x_at = [lax.rem(x + k, xs) for k in range(xs)]
    y_at = [y, 1 - y]
    z_at = [lax.rem(z + k, depth) for k in range(depth)]
    core_at = [core, 1 - core]
    z_steps = sorted(range(depth), key=lambda k: -away(k, depth))
    z_ids = [z_at[k] * CORES + core for k in z_steps[:-1]]
    team_ids = [z_at[k] * CORES + core_at[c] for k in z_steps for c in (1, 0)]
    by_core_ids = [z_at[k] * CORES + core_at[c] for c in (1, 0) for k in z_steps]
    fixed_core_ids = [z_at[k] * CORES + c for c in range(CORES) for k in z_steps]
    chip_steps = sorted(
        [(j, i) for j in range(Y_LO) for i in range(xs) if (j, i) != (0, 0)],
        key=lambda k: -k[0] - away(k[1], xs),
    )
    chip_ids = [y_at[j] * xs + x_at[i] for j, i in chip_steps]

    def at_core(there_core):
        return z * CORES + there_core

    def remote(src, dst, which, device):
        return pltpu.make_async_remote_copy(
            src_ref=src,
            dst_ref=dst,
            send_sem=send.at[which],
            recv_sem=recv.at[which],
            device_id=device,
            device_id_type=MESH,
        )

    def landed(block, which):
        pltpu.make_async_copy(block, block, recv.at[which]).wait()

    def sent(block, which):
        pltpu.make_async_copy(block, block, send.at[which]).wait()

    def columns(there):
        return jac.at[:, pl.ds(pl.multiple_of(there * width, width), width)]

    barrier = pltpu.get_barrier_semaphore()

    def greet(device):
        pl.semaphore_signal(barrier, inc=1, device_id=device, device_id_type=MESH)

    @pl.when(worker)
    def _():
        for there in team_ids:
            greet((there + team, p))
        for there in team_ids[:-1]:
            greet((there, p))
        each(par - 1, lambda k: greet((s, lax.rem(p + 1 + k, par))))

    def stage(there):
        pltpu.make_async_copy(columns(there), jown.at[there], local.at[0]).start()

    each(team, stage)
    level_copy = pltpu.make_async_copy(energies, elist, local.at[1])
    level_copy.start()
    level_copy.wait()
    lane = lax.broadcasted_iota(jnp.int32, (1, LANES), 1)
    offset = lax.rem(s * rows, LANES)
    mine = jnp.zeros((1, LANES), jnp.float32)
    for r in range(rows):
        mine = jnp.where(lane == offset + r, elist[r], mine)
    eown[...] = mine
    pltpu.make_async_copy(jown, jown, local.at[0]).wait()

    def give_rows(there):
        remote(jown.at[there], jbuf.at[s], 0, (there, p)).start()

    def give_energies(there):
        remote(eown, ebuf.at[s], 1, (there, p)).start()

    def work():
        block = jbuf[...].reshape(count, width)
        mean_col = total_rows(block) / count
        scaled = ((block - mean_col) * (1.0 / P_SIZE**0.5)).astype(jnp.bfloat16)
        scaled_ref[...] = scaled.astype(jnp.float32)
        part = lax.dot_general(
            scaled, scaled, (((1,), (1,)), ((), ())), preferred_element_type=jnp.float32
        )
        gpart[...] = part.reshape(gpart.shape)

        def scatter(there):
            remote(gpart.at[there], rs.at[rank], 2, (at_core(0), there)).start()
            remote(
                gpart.at[chips + there, :, right], rs.at[rank, :, right], 2, (at_core(1), there)
            ).start()

        for there in chip_ids:
            scatter(there)

        @pl.when(core == 0)
        def _():
            remote(gpart.at[chips + p, :, right], rs.at[rank, :, right], 2, (at_core(1), p)).start()

        @pl.when(core == 1)
        def _():
            remote(gpart.at[p], rs.at[rank], 2, (at_core(0), p)).start()

        rs[rank] = gpart[rank]
        for there in team_ids[:-1]:
            give_energies(there)

        others = pl.ds(0, 2 * chips - 1)
        z_others = pl.ds(0, depth - 1)
        every = pl.ds(0, count)

        def across_z(part_of):
            landed(rs.at[others, :, part_of], 2)
            ar[z, :, part_of] = jnp.sum(rs[:, :, part_of], axis=0)
            for there in z_ids:
                remote(ar.at[z, :, part_of], ar.at[z, :, part_of], 3, (there, p)).start()

        def spread(part_of, mine_of, which):
            landed(ar.at[z_others, :, part_of], 3)
            mine_of[p] = jnp.sum(ar[:, :, part_of], axis=0)
            for there_core in range(CORES):
                for there in chip_ids:
                    remote(mine_of.at[p], mine_of.at[p], which, (at_core(there_core), there)).start()
            remote(mine_of.at[p], mine_of.at[p], which, (at_core(1 - core), p)).start()

        @pl.when(core == 0)
        def _():
            across_z(every)

        @pl.when(core == 1)
        def _():
            across_z(right)

        landed(ebuf.at[pl.ds(0, samp - 1)], 1)
        level = jnp.concatenate(
            [jnp.sum(ebuf[i * per : (i + 1) * per], axis=0) for i in range(samp // per)], axis=1
        )
        right_row = total_lanes(level) / count - level
        diagonal = lax.broadcasted_iota(jnp.int32, (count, count), 0) == lax.broadcasted_iota(
            jnp.int32, (count, count), 1
        )
        right_col = total_lanes(jnp.where(diagonal, right_row, 0.0))

        @pl.when(core == 0)
        def _():
            spread(every, top, 4)
            landed(top.at[pl.ds(0, chips - 1)], 4)
            landed(low, 5)

        @pl.when(core == 1)
        def _():
            spread(right, low, 5)
            landed(top, 4)
            landed(low.at[pl.ds(0, chips - 1)], 5)

        above = top[...].reshape(half, count)
        g_aa, g_ab = above[:, :half], above[:, half:]
        g_bb = low[...].reshape(half, half)
        g_ba = jnp.transpose(g_ab)
        cols = [right_col[:half], right_col[half:]]
        rows_of = [right_row[:, :half], right_row[:, half:]]
        d_row, r_row, d_col, r_col = rows_of, rows_of, cols, cols
        c_row = [jnp.zeros_like(v) for v in rows_of]
        c_col = [jnp.zeros_like(v) for v in cols]

        def inner(u, v):
            return total_lanes(u[0] * v[0] + u[1] * v[1])

        rr = inner(r_row, r_row)
        for turn in range(ITERS):
            image_row = [
                total_rows(g_aa * d_col[0] + g_ba * d_col[1]) + SHIFT * d_row[0],
                total_rows(g_ab * d_col[0] + g_bb * d_col[1]) + SHIFT * d_row[1],
            ]
            size = rr / inner(d_row, image_row)
            c_row = [c + size * d for c, d in zip(c_row, d_row)]
            c_col = [c + size * d for c, d in zip(c_col, d_col)]
            if turn == ITERS - 1:
                break
            image_col = [
                total_lanes(g_aa * d_row[0] + g_ab * d_row[1]) + SHIFT * d_col[0],
                total_lanes(g_ba * d_row[0] + g_bb * d_row[1]) + SHIFT * d_col[1],
            ]
            r_row = [r - size * v for r, v in zip(r_row, image_row)]
            r_col = [r - size * v for r, v in zip(r_col, image_col)]
            fresh = inner(r_row, r_row)
            ratio = fresh / rr
            d_row = [r + ratio * d for r, d in zip(r_row, d_row)]
            d_col = [r + ratio * d for r, d in zip(r_col, d_col)]
            rr = fresh

        c_row = jnp.concatenate(c_row, axis=1)

        update[s] = total_rows(scaled_ref[:half] * c_col[0] + scaled_ref[half:] * c_col[1])

        def give_piece(there):
            remote(update.at[s], update.at[s], 6, (there, p)).start()

        for there in [z_at[k] * CORES + c for c in reversed(range(CORES)) for k in z_steps]:

            @pl.when(there != s)
            def _(there=there):
                give_piece(there)

            give_piece(there + team)


        def own_samples(first):
            here = lax.rem(s, team) // per
            piece = c_row[:, first : first + LANES]
            for i in range(1, team // per):
                piece = jnp.where(here == i, c_row[:, first + i * LANES : first + (i + 1) * LANES], piece)
            return pltpu.roll(piece, lax.rem(LANES - offset, LANES), 1)

        cown[...] = own_samples(half)
        remote(cown, cbuf, 7, (s + team, p)).start()
        coeffs[...] = own_samples(0)[0, :rows]

        sent(jbuf.at[pl.ds(0, team - 1)], 0)
        sent(ebuf.at[pl.ds(0, team - 1)], 1)

        @pl.when(core == 0)
        def _():
            sent(gpart.at[pl.ds(0, chips - 1)], 2)
            sent(gpart.at[pl.ds(0, chips), :, right], 2)
            sent(ar.at[z_others], 3)
            sent(rs.at[others], 4)

        @pl.when(core == 1)
        def _():
            sent(gpart.at[pl.ds(0, chips)], 2)
            sent(gpart.at[pl.ds(0, chips - 1), :, right], 2)
            sent(ar.at[z_others, :, right], 3)
            sent(rs.at[others, :, right], 5)

        sent(update, 6)
        sent(update.at[pl.ds(0, team - 1)], 6)
        sent(cown, 7)
        landed(update.at[pl.ds(0, team - 1)], 6)


    @pl.when(sender)
    def _():
        pl.semaphore_wait(barrier, team)
        for there in fixed_core_ids:
            give_rows(there)
        sent(jbuf.at[pl.ds(0, team)], 0)
        for there in team_ids:
            give_energies(there)
        landed(cbuf, 7)
        coeffs[...] = cbuf[...][0, :rows]
        sent(ebuf.at[pl.ds(0, team)], 1)
        landed(update, 6)

    @pl.when(worker)
    def _():
        pl.semaphore_wait(barrier, team - 1 + par - 1)
        for there in fixed_core_ids:

            @pl.when(there != s)
            def _(there=there):
                give_rows(there)

        ebuf[s] = mine
        jbuf[s] = jown[s]
        landed(jbuf.at[pl.ds(0, samp - 1)], 0)
        work()


def hand_over_kernel(update, coeffs, update_out, coeffs_out, done):
    first = pltpu.make_async_copy(update, update_out, done.at[0])
    second = pltpu.make_async_copy(coeffs, coeffs_out, done.at[1])
    first.start()
    second.start()
    first.wait()
    second.wait()


def hand_over(update, coeffs):
    anywhere = pl.BlockSpec(memory_space=pl.ANY)
    return pl.pallas_call(
        hand_over_kernel,
        out_shape=(
            jax.ShapeDtypeStruct(update.shape, update.dtype),
            jax.ShapeDtypeStruct(coeffs.shape, coeffs.dtype),
        ),
        in_specs=[anywhere, anywhere],
        out_specs=(anywhere, anywhere),
        scratch_shapes=[pltpu.SemaphoreType.DMA((2,))],
        compiler_params=pltpu.CompilerParams(vmem_limit_bytes=VMEM_BYTES),
    )(update, coeffs)


def solution(mesh):
    samp, par = mesh.shape["samp"], mesh.shape["par"]
    chips = par
    depth = samp // (CORES * Y_HI)
    team = samp // Y_HI

    def per_device(jacobian, energies):
        rows, columns = jacobian.shape
        width = columns // team
        count = rows * samp
        half = count // 2
        share = half // chips
        update, coeffs = pl.pallas_call(
            functools.partial(kernel, samp, par),
            out_shape=(
                jax.ShapeDtypeStruct((team, 1, width), jnp.float32),
                jax.ShapeDtypeStruct((rows,), jnp.float32),
            ),
            in_specs=[
                pl.BlockSpec(memory_space=pl.ANY),
                pl.BlockSpec(memory_space=pl.ANY),
            ],
            out_specs=(
                pl.BlockSpec(memory_space=pltpu.VMEM),
                pl.BlockSpec(memory_space=pltpu.VMEM),
            ),
            scratch_shapes=[
                pltpu.VMEM((team, rows, width), jnp.float32),
                pltpu.SMEM((rows,), jnp.float32),
                pltpu.VMEM((samp, rows, width), jnp.float32),
                pltpu.VMEM((samp, 1, LANES), jnp.float32),
                pltpu.VMEM((1, LANES), jnp.float32),
                pltpu.VMEM((count, width), jnp.float32),
                pltpu.VMEM((2 * chips, share, count), jnp.float32),
                pltpu.VMEM((2 * chips, share, count), jnp.float32),
                pltpu.VMEM((depth, share, count), jnp.float32),
                pltpu.VMEM((chips, share, count), jnp.float32),
                pltpu.VMEM((chips, share, half), jnp.float32),
                pltpu.VMEM((1, LANES), jnp.float32),
                pltpu.VMEM((1, LANES), jnp.float32),
                pltpu.SemaphoreType.DMA((8,)),
                pltpu.SemaphoreType.DMA((8,)),
                pltpu.SemaphoreType.DMA((2,)),
            ],
            compiler_params=pltpu.CompilerParams(
                collective_id=0, has_side_effects=True, vmem_limit_bytes=VMEM_BYTES
            ),
        )(
            pltpu.with_memory_space_constraint(jacobian, pltpu.HBM),
            pltpu.with_memory_space_constraint(energies, pltpu.HBM),
        )
        return hand_over(update.reshape(columns), coeffs)

    return jax.shard_map(
        per_device,
        mesh=mesh,
        in_specs=(P("samp", "par"), P("samp")),
        out_specs=(P("par"), P("samp")),
        check_vma=False,
    )
```
